32 devices in a mesh: section: 8 (over y, x, core), expert: 4 (over z).
Axes of the slice: x: 2, y: 2, z: 4, core: 2. Of those that a mesh axis runs over, the one named last changes fastest.
Arguments:
- forward_input: bfloat16 [8, 512, 2048], P('section', 'expert'), may hold values from -6 to 6
- forward_routes: int32 [8, 512, 8], P('section', 'expert'), may hold values from 0 to 127, as said below
- forward_shares: float32 [8, 512, 8], P('section', 'expert'), may hold values from 0.1 to 1
- backward_input: bfloat16 [8, 512, 2048], P('section', 'expert'), may hold values from -6 to 6
- backward_routes: int32 [8, 512, 8], P('section', 'expert'), may hold values from 0 to 127, as said below
- backward_shares: float32 [8, 512, 8], P('section', 'expert'), may hold values from 0.1 to 1
- output_grad: bfloat16 [8, 512, 2048], P('section', 'expert'), may hold values from -6 to 6
- norm_gain: float32 [8, 2048], P('section'), may hold values from 0.5 to 1.5
- gate_weight: bfloat16 [8, 3072, 2048], P('section', 'expert'), may hold values from -0.125 to 0.125
- up_weight: bfloat16 [8, 3072, 2048], P('section', 'expert'), may hold values from -0.125 to 0.125
- down_weight: bfloat16 [8, 3072, 2048], P('section', 'expert'), may hold values from -0.15625 to 0.15625
Outputs:
- next_input: bfloat16 [8, 512, 2048], P('section', 'expert')
- previous_gradient: bfloat16 [8, 512, 2048], P('section', 'expert')
The draws below stay inside these ranges and needn't reach their ends.
Inputs may be any that keep to these rules, and one draw needn't show every extreme that they name: `forward_routes`: each token names 8 different experts. Among the 128 tokens of one device, at most 16 name any one expert below 2; in every draw some section has every device sending exactly 16 tokens to one expert below 2. `backward_routes`: as for forward_routes.
All inputs are finite; a program needn't handle non-finite values.
Results may differ from the reference program's by a relative error of at most 0.007.
Values may be sent and summed in bfloat16 or wider, within the bound.
No kernel may reach another device: no remote copies, remote signals or barrier semaphores. Data moves between devices by JAX's collectives and lax.ppermute only.
A program may use at most 64 MiB of HBM per device.

```python
import math
import jax
import jax.numpy as jnp
from jax import lax

D = 2048
HIDDEN_SIZE = 1536
EXPERTS = 128
TOPK = 8
EF = 2
TOK_DEV = 128
CAP = 16
TOKENS = 512
N_SECTION = 8
N_EXPERT = 4


def routes_for(key):
    keys = jax.random.split(key, 6)
    counts = jax.random.randint(keys[0], (N_SECTION, N_EXPERT, EF), CAP // 2, CAP + 1)
    full_section = jax.random.randint(keys[1], (), 0, N_SECTION)
    full_expert = jax.random.randint(keys[2], (), 0, EF)
    section_index = jnp.arange(N_SECTION)[:, None, None]
    expert_index = jnp.arange(EF)[None, None, :]
    counts = jnp.where((section_index == full_section) & (expert_index == full_expert), CAP, counts)
    scores = jax.random.randint(keys[3], (N_SECTION, N_EXPERT, EF, TOK_DEV), 0, 1 << 20) * TOK_DEV + jnp.arange(TOK_DEV)
    ranks = jnp.argsort(jnp.argsort(scores, axis=-1), axis=-1)
    member = ranks < counts[..., None]
    member = jnp.transpose(member, (0, 1, 3, 2)).reshape(N_SECTION, N_EXPERT * TOK_DEV, EF)
    other_scores = jax.random.randint(keys[4], (N_SECTION, N_EXPERT * TOK_DEV, EXPERTS - EF), 0, 1 << 16)
    other_scores = other_scores * (EXPERTS - EF) + jnp.arange(EXPERTS - EF)
    others = lax.top_k(other_scores, TOPK)[1] + EF
    running = jnp.cumsum(member.astype(jnp.int32), axis=-1)
    held = running[..., -1:]
    place = jnp.arange(TOPK)
    chosen = member[..., None, :] & (running[..., None, :] == place[:, None] + 1)
    hosted_at = jnp.sum(jnp.where(chosen, jnp.arange(EF), 0), axis=-1)
    routes = jnp.where(place < held, hosted_at, others)
    turn = jax.random.randint(keys[5], (N_SECTION, N_EXPERT * TOK_DEV, 1), 0, TOPK)
    return jnp.take_along_axis(routes, (place + turn) % TOPK, axis=-1).astype(jnp.int32)


def draw_forward_routes(key, part):
    return routes_for(jax.random.fold_in(key, 11))


def draw_backward_routes(key, part):
    return routes_for(jax.random.fold_in(key, 23))


def block_levels(own_key, extent, shards, smallest, high):
    def one(dim, parts):
        draws = jax.random.uniform(jax.random.fold_in(jax.random.fold_in(own_key, 6), dim), (parts,), jnp.float32, smallest / len(shards), high / len(shards))
        return jnp.repeat(jnp.exp(draws), extent[dim] // parts).reshape((-1,) + (1,) * (len(extent) - dim - 1))

    level = one(*shards[0])
    for cut in shards[1:]:
        level = level * one(*cut)
    return level


def centred(key, extent, deviation, most, pieces=(), held_as=jnp.bfloat16):
    array = deviation * jax.random.normal(key, extent, jnp.float32)
    if pieces:
        array = array * block_levels(key, extent, pieces, -0.22, 0.18)
    return jnp.clip(array, -most, most).astype(held_as)


def setup_inputs(seed: int = 0) -> dict:
    key_list = jax.random.split(jax.random.key(seed), 12)
    return {
        "forward_input": centred(key_list[0], (N_SECTION, TOKENS, D), 1.0, 6.0, ((0, 8), (1, 4))),
        "forward_routes": draw_forward_routes(jax.random.fold_in(key_list[11], 71), 0),
        "forward_shares": jnp.clip(jnp.exp(math.log(1.0) - 2.3025851 * jax.random.uniform(key_list[2], (N_SECTION, TOKENS, TOPK), jnp.float32) ** block_levels(key_list[2], (N_SECTION, TOKENS, TOPK), ((0, 8), (1, 4)), -0.2, 0.2)), 0.1, 1.0),
        "backward_input": centred(key_list[3], (N_SECTION, TOKENS, D), 1.0, 6.0, ((0, 8), (1, 4))),
        "backward_routes": draw_backward_routes(jax.random.fold_in(key_list[11], 71), 0),
        "backward_shares": jnp.clip(jnp.exp(math.log(1.0) - 2.3025851 * jax.random.uniform(key_list[5], (N_SECTION, TOKENS, TOPK), jnp.float32) ** block_levels(key_list[5], (N_SECTION, TOKENS, TOPK), ((0, 8), (1, 4)), -0.2, 0.2)), 0.1, 1.0),
        "output_grad": centred(key_list[6], (N_SECTION, TOKENS, D), 1.0, 6.0, ((0, 8), (1, 4))),
        "norm_gain": jnp.clip(1.0 + 0.1 * jax.random.normal(key_list[7], (N_SECTION, D), jnp.float32), 0.5, 1.5),
        "gate_weight": centred(key_list[8], (N_SECTION, EF * HIDDEN_SIZE, D), D ** -0.5, 0.125, ((0, 8), (1, 4))),
        "up_weight": centred(key_list[9], (N_SECTION, EF * HIDDEN_SIZE, D), D ** -0.5, 0.125, ((0, 8), (1, 4))),
        "down_weight": centred(key_list[10], (N_SECTION, EF * HIDDEN_SIZE, D), HIDDEN_SIZE ** -0.5, 0.15625, ((0, 8), (1, 4))),
    }


EPSILON = 1e-06

def route_tables(route_ids, shares):
    hosted = jnp.arange(EF, dtype=jnp.int32)
    match = route_ids[:, :, None] == hosted
    member = jnp.any(match, axis=1)
    weight = lax.optimization_barrier(jnp.sum(jnp.where(match, shares[:, :, None], 0.0), axis=1))
    member_int = member.astype(jnp.int32)
    rank = jnp.cumsum(member_int, axis=0) - member_int
    slots = jnp.arange(CAP, dtype=jnp.int32)
    placed = member.T[:, None, :] & (rank.T[:, None, :] == slots[None, :, None])
    table = placed.astype(jnp.float32)
    return (table, table * weight.T[:, None, :])

def normalize(rows, gain):
    values = rows.astype(jnp.float32)
    scale = lax.rsqrt(lax.optimization_barrier(jnp.mean(values * values, axis=-1, keepdims=True)) + EPSILON)
    unit = values * scale
    return (unit, scale, (unit * gain).astype(jnp.bfloat16))

def slice_forward(slots_in, gate_rows, up_rows, down_rows):
    gate = jnp.dot(slots_in, gate_rows.T, preferred_element_type=jnp.float32)
    upper = jnp.dot(slots_in, up_rows.T, preferred_element_type=jnp.float32)
    hidden = (jax.nn.silu(gate) * upper).astype(jnp.bfloat16)
    return jnp.dot(hidden, down_rows, preferred_element_type=jnp.float32).astype(jnp.bfloat16)

def slice_backward(slots_in, slot_grad, gate_rows, up_rows, down_rows):
    gate = jnp.dot(slots_in, gate_rows.T, preferred_element_type=jnp.float32)
    upper = jnp.dot(slots_in, up_rows.T, preferred_element_type=jnp.float32)
    sigma = jax.nn.sigmoid(gate)
    hidden_grad = jnp.dot(slot_grad, down_rows.T, preferred_element_type=jnp.float32)
    gate_grad = (hidden_grad * upper * sigma * (1.0 + gate * (1.0 - sigma))).astype(jnp.bfloat16)
    upper_grad = (hidden_grad * gate * sigma).astype(jnp.bfloat16)
    total = jnp.dot(gate_grad, gate_rows, preferred_element_type=jnp.float32)
    total = total + jnp.dot(upper_grad, up_rows, preferred_element_type=jnp.float32)
    return total.astype(jnp.bfloat16)

def to_slots(table, rows):
    blocks = rows.astype(jnp.float32).reshape(N_EXPERT, TOK_DEV, D)
    return jnp.einsum('nect,ntd->necd', table, blocks, precision=lax.Precision.HIGHEST).astype(jnp.bfloat16)

def one_section(operands):
    forward_rows, forward_ids, forward_weights, backward_rows, backward_ids, backward_weights, grad_rows, gain, gate_all, up_all, down_all = operands
    group = N_EXPERT // EF
    width = HIDDEN_SIZE * EF // N_EXPERT
    forward_unit, forward_scale, forward_normed = normalize(forward_rows, gain)
    backward_unit, backward_scale, backward_normed = normalize(backward_rows, gain)
    forward_table, forward_weighted = jax.vmap(route_tables)(forward_ids.reshape(N_EXPERT, TOK_DEV, TOPK), forward_weights.reshape(N_EXPERT, TOK_DEV, TOPK))
    backward_table, backward_weighted = jax.vmap(route_tables)(backward_ids.reshape(N_EXPERT, TOK_DEV, TOPK), backward_weights.reshape(N_EXPERT, TOK_DEV, TOPK))
    forward_slots = to_slots(forward_table, forward_normed)
    backward_slots = to_slots(backward_table, backward_normed)
    grad_slots = to_slots(backward_weighted, grad_rows)
    forward_out = []
    backward_out = []
    for expert in range(EF):
        slots_f = forward_slots[:, expert].reshape(N_EXPERT * CAP, D)
        slots_b = backward_slots[:, expert].reshape(N_EXPERT * CAP, D)
        slots_g = grad_slots[:, expert].reshape(N_EXPERT * CAP, D)
        total_f = jnp.zeros((N_EXPERT * CAP, D), jnp.float32)
        total_b = jnp.zeros((N_EXPERT * CAP, D), jnp.float32)
        for piece in range(group):
            start = (expert * group + piece) * width
            gate_rows = gate_all[start:start + width]
            up_rows = up_all[start:start + width]
            down_rows = down_all[start:start + width]
            total_f = total_f + slice_forward(slots_f, gate_rows, up_rows, down_rows).astype(jnp.float32)
            total_b = total_b + slice_backward(slots_b, slots_g, gate_rows, up_rows, down_rows).astype(jnp.float32)
        forward_out.append(total_f.reshape(N_EXPERT, CAP, D))
        backward_out.append(total_b.reshape(N_EXPERT, CAP, D))
    forward_result = jnp.stack(forward_out, axis=1)
    backward_result = jnp.stack(backward_out, axis=1)
    mixed = jnp.einsum('nect,necd->ntd', forward_weighted, forward_result, precision=lax.Precision.HIGHEST).reshape(TOKENS, D)
    next_rows = (forward_rows.astype(jnp.float32) + mixed).astype(jnp.bfloat16)
    normed_grad = jnp.einsum('nect,necd->ntd', backward_table, backward_result, precision=lax.Precision.HIGHEST).reshape(TOKENS, D)
    scaled = normed_grad * gain
    input_grad = backward_scale * (scaled - backward_unit * lax.optimization_barrier(jnp.mean(scaled * backward_unit, axis=-1, keepdims=True)))
    previous_rows = (grad_rows.astype(jnp.float32) + input_grad).astype(jnp.bfloat16)
    return (next_rows, previous_rows)

def reference(forward_input, forward_routes, forward_shares, backward_input, backward_routes, backward_shares, output_grad, norm_gain, gate_weight, up_weight, down_weight):
    next_rows, previous_rows = lax.map(one_section, (forward_input, forward_routes, forward_shares, backward_input, backward_routes, backward_shares, output_grad, norm_gain, gate_weight, up_weight, down_weight))
    return (jnp.roll(next_rows, 1, axis=0), jnp.roll(previous_rows, -1, axis=0))
```

```python
import functools

import jax
import jax.numpy as jnp
from jax import lax
from jax.experimental import pallas as pl
from jax.experimental.pallas import tpu as pltpu
from jax.sharding import PartitionSpec as P

EF = 2
CAP = 16
EPSILON = 1e-06
LANES = 128
MIB = 1 << 20

VMEM = pl.BlockSpec(memory_space=pltpu.VMEM)
SMEM = pl.BlockSpec(memory_space=pltpu.SMEM)


def call(body, outs, specs, flops, nbytes, limit):
    return pl.pallas_call(
        body,
        out_shape=outs,
        in_specs=specs,
        out_specs=[VMEM] * len(outs),
        compiler_params=pltpu.CompilerParams(vmem_limit_bytes=limit * MIB),
        cost_estimate=pl.CostEstimate(flops=flops, bytes_accessed=nbytes, transcendentals=0),
    )


def bf16(shape):
    return jax.ShapeDtypeStruct(shape, jnp.bfloat16)


def slot_tables(owner, routes, shares):
    tokens = routes.shape[0]
    lane = lax.broadcasted_iota(jnp.int32, (tokens, LANES), 1)
    weights = []
    members = []
    for expert in (owner, 1 - owner):
        hit = routes == expert
        members.append(jnp.sum(jnp.where(hit, 1.0, 0.0), axis=1, keepdims=True))
        weights.append(jnp.sum(jnp.where(hit, shares, 0.0), axis=1, keepdims=True))
    first = lane < CAP
    used = lane < EF * CAP
    member = jnp.where(used, jnp.where(first, members[0], members[1]), 0.0)
    row = lax.broadcasted_iota(jnp.int32, (tokens, tokens), 0)
    col = lax.broadcasted_iota(jnp.int32, (tokens, tokens), 1)
    earlier = jnp.where(col < row, 1.0, 0.0).astype(jnp.bfloat16)
    rank = jnp.dot(earlier, member.astype(jnp.bfloat16), preferred_element_type=jnp.float32)
    slot = (lane % CAP).astype(jnp.float32)
    placed = jnp.where((member > 0.5) & (rank == slot), 1.0, 0.0)
    return lane, first, weights, placed


def dispatch_forward(owner_ref, routes_ref, shares_ref, rows_ref, own_ref, other_ref, early_ref):
    lane, first, weights, placed = slot_tables(owner_ref[0], routes_ref[0], shares_ref[0])
    rows = rows_ref[0]
    width = rows.shape[1]
    table = placed
    for e, weight in enumerate(weights):
        left = weight
        for piece in range(3):
            part = left.astype(jnp.bfloat16).astype(jnp.float32)
            left = left - part
            table = jnp.where(lane == EF * CAP + 3 * e + piece, part, table)
    early_ref[:, width:] = table.astype(jnp.bfloat16)
    early_ref[:, :width] = rows
    pick = jnp.transpose(placed)[: EF * CAP].astype(jnp.bfloat16)
    slots = jnp.dot(pick, rows, preferred_element_type=jnp.float32).astype(jnp.bfloat16)
    own_ref[...] = slots[:CAP]
    other_ref[...] = slots[CAP:]


def dispatch_backward(
    owner_ref, routes_ref, shares_ref, rows_ref, grad_ref, own_ref, other_ref, early_ref
):
    lane, first, weights, placed = slot_tables(owner_ref[0], routes_ref[0], shares_ref[0])
    rows = rows_ref[0]
    grads = grad_ref[0]
    width = rows.shape[1]
    turned = jnp.transpose(placed)[: EF * CAP]
    shared = jnp.transpose(placed * jnp.where(first, weights[0], weights[1]))[: EF * CAP]
    share = jnp.sum(shared, axis=1, keepdims=True)
    pick = turned.astype(jnp.bfloat16)
    slots = jnp.dot(pick, rows, preferred_element_type=jnp.float32).astype(jnp.bfloat16)
    picked = jnp.dot(pick, grads, preferred_element_type=jnp.float32)
    grad_slots = (share * picked).astype(jnp.bfloat16)
    own_ref[:CAP] = slots[:CAP]
    own_ref[CAP:] = grad_slots[:CAP]
    other_ref[:CAP] = slots[CAP:]
    other_ref[CAP:] = grad_slots[CAP:]
    early_ref[:, width:] = placed.astype(jnp.bfloat16)
    early_ref[:, :width] = grads


def project(left, right):
    return lax.dot_general(
        left, right, (((1,), (1,)), ((), ())), preferred_element_type=jnp.float32
    )


def unit_rows(rows):
    values = rows.astype(jnp.float32)
    scale = lax.rsqrt(jnp.mean(values * values, axis=-1, keepdims=True) + EPSILON)
    return values * scale, scale


def expert_forward(blocks, *refs):
    rows = jnp.concatenate([ref[...] for ref in refs[:blocks]], axis=0)
    gain_ref, gate_ref, up_ref, down_ref = refs[blocks : blocks + 4]
    outs = refs[blocks + 4 :]
    unit, _ = unit_rows(rows)
    normed = (unit * gain_ref[...]).astype(jnp.bfloat16)
    gate = project(normed, gate_ref[0])
    upper = project(normed, up_ref[0])
    hidden = (gate * jax.nn.sigmoid(gate) * upper).astype(jnp.bfloat16)
    result = jnp.dot(hidden, down_ref[0], preferred_element_type=jnp.float32)
    result = result.astype(jnp.bfloat16)
    for k in range(blocks):
        outs[k][...] = result[k * CAP : (k + 1) * CAP]


def expert_backward(blocks, *refs):
    rows = jnp.concatenate([ref[:CAP] for ref in refs[:blocks]], axis=0)
    grads = jnp.concatenate([ref[CAP:] for ref in refs[:blocks]], axis=0)
    gain_ref, gate_ref, up_ref, down_ref = refs[blocks : blocks + 4]
    outs = refs[blocks + 4 :]
    gain = gain_ref[...]
    unit, scale = unit_rows(rows)
    normed = (unit * gain).astype(jnp.bfloat16)
    hidden_grad = project(grads, down_ref[0])
    gate = project(normed, gate_ref[0])
    upper = project(normed, up_ref[0])
    sigma = jax.nn.sigmoid(gate)
    gate_grad = (hidden_grad * upper * sigma * (1.0 + gate * (1.0 - sigma))).astype(jnp.bfloat16)
    upper_grad = (hidden_grad * gate * sigma).astype(jnp.bfloat16)
    total = jnp.dot(gate_grad, gate_ref[0], preferred_element_type=jnp.float32)
    total = total + jnp.dot(upper_grad, up_ref[0], preferred_element_type=jnp.float32)
    scaled = total * gain
    inner = jnp.mean(scaled * unit, axis=-1, keepdims=True)
    result = (scale * (scaled - unit * inner)).astype(jnp.bfloat16)
    for k in range(blocks):
        outs[k][...] = result[k * CAP : (k + 1) * CAP]


def combine_forward(half, early_ref, *refs):
    out_ref = refs[-1]
    width = out_ref.shape[2]
    total = early_ref[:, :width].astype(jnp.float32)
    table = early_ref[:, width:]
    for e in range(EF):
        parts = jnp.concatenate([ref[...] for ref in refs[e * half : (e + 1) * half]], axis=0)
        pick = jnp.concatenate([table[:, e * CAP : (e + 1) * CAP]] * half, axis=1)
        column = EF * CAP + 3 * e
        weight = jnp.sum(
            table[:, column : column + 3].astype(jnp.float32), axis=1, keepdims=True
        )
        total = total + weight * jnp.dot(pick, parts, preferred_element_type=jnp.float32)
    out_ref[0] = total.astype(jnp.bfloat16)


def combine_backward(half, early_ref, *refs):
    out_ref = refs[-1]
    width = out_ref.shape[2]
    table = early_ref[:, width:]
    parts = jnp.concatenate([ref[...] for ref in refs[:-1]], axis=0)
    pick = jnp.concatenate(
        [table[:, e * CAP : (e + 1) * CAP] for e in range(EF) for _ in range(half)], axis=1
    )
    total = early_ref[:, :width].astype(jnp.float32)
    total = total + jnp.dot(pick, parts, preferred_element_type=jnp.float32)
    out_ref[0] = total.astype(jnp.bfloat16)


def on_device(
    sections,
    devices,
    forward_input,
    forward_routes,
    forward_shares,
    backward_input,
    backward_routes,
    backward_shares,
    output_grad,
    norm_gain,
    gate_weight,
    up_weight,
    down_weight,
):
    half = devices // EF
    tokens, width = forward_input.shape[1:]
    hidden = gate_weight.shape[1]
    owner = (lax.axis_index("expert") // half).astype(jnp.int32)[None]

    def swapped(block, k):
        return lax.ppermute(block, "expert", [(i, i ^ k) for i in range(devices)])

    def moved(block, distance):
        route = [(i, (i + distance) % sections) for i in range(sections)]
        return lax.ppermute(block, "section", route)

    def returned(block, distance, k):
        route = [
            (s * devices + z, (s + distance) % sections * devices + (z ^ k))
            for s in range(sections)
            for z in range(devices)
        ]
        return lax.ppermute(block, ("section", "expert"), route)

    def gathered(own, other):
        blocks = [own]
        far = [swapped(other, half)]
        step = 1
        while step < half:
            blocks = blocks + [swapped(b, step) for b in blocks]
            far = far + [swapped(b, step) for b in far]
            step *= 2
        return blocks + far

    dispatch_bytes = 3 * tokens * width * 2
    own_b, other_b, early_b = call(
        dispatch_backward,
        [bf16((2 * CAP, width)), bf16((2 * CAP, width)), bf16((tokens, width + LANES))],
        [SMEM, VMEM, VMEM, VMEM, VMEM],
        4 * EF * CAP * tokens * width,
        dispatch_bytes,
        24,
    )(owner, backward_routes, backward_shares, backward_input, output_grad)
    own_f, other_f, early_f = call(
        dispatch_forward,
        [bf16((CAP, width)), bf16((CAP, width)), bf16((tokens, width + LANES))],
        [SMEM, VMEM, VMEM, VMEM],
        2 * EF * CAP * tokens * width,
        dispatch_bytes,
        24,
    )(owner, forward_routes, forward_shares, forward_input)

    blocks_b = gathered(own_b, other_b)
    blocks_f = gathered(own_f, other_f)
    early_b = moved(early_b, -1)
    early_f = moved(early_f, 1)

    weights = [
        pltpu.with_memory_space_constraint(w, pltpu.VMEM)
        for w in (gate_weight, up_weight, down_weight)
    ]
    rows = devices * CAP
    weight_bytes = 3 * hidden * width * 2
    outs = [bf16((CAP, width))] * devices
    parts_b = call(
        functools.partial(expert_backward, devices),
        outs,
        [VMEM] * (devices + 4),
        10 * rows * hidden * width,
        weight_bytes,
        24,
    )(*blocks_b, norm_gain, *weights)
    parts_f = call(
        functools.partial(expert_forward, devices),
        outs,
        [VMEM] * (devices + 4),
        6 * rows * hidden * width,
        weight_bytes,
        24,
    )(*blocks_f, norm_gain, *weights)

    parts_b = [returned(part, -1, k) for k, part in enumerate(parts_b)]
    parts_f = [returned(part, 1, k) for k, part in enumerate(parts_f)]
    result = [bf16((1, tokens, width))]
    (previous_gradient,) = call(
        functools.partial(combine_backward, half),
        result,
        [VMEM] * (devices + 1),
        2 * tokens * devices * CAP * width,
        dispatch_bytes,
        24,
    )(early_b, *parts_b)
    (next_input,) = call(
        functools.partial(combine_forward, half),
        result,
        [VMEM] * (devices + 1),
        2 * tokens * devices * CAP * width,
        dispatch_bytes,
        24,
    )(early_f, *parts_f)
    return next_input, previous_gradient


def solution(mesh):
    rows = P("section", "expert", None)
    return jax.shard_map(
        functools.partial(on_device, mesh.shape["section"], mesh.shape["expert"]),
        mesh=mesh,
        in_specs=(rows,) * 7 + (P("section", None),) + (rows,) * 3,
        out_specs=(rows, rows),
        check_vma=False,
    )
```

```python
import functools

import jax
import jax.numpy as jnp
from jax import lax
from jax.experimental import pallas as pl
from jax.experimental.pallas import tpu as pltpu
from jax.sharding import PartitionSpec as P

EF = 2
CAP = 16
EPSILON = 1e-06
LANES = 128
MIB = 1 << 20

VMEM = pl.BlockSpec(memory_space=pltpu.VMEM)
SMEM = pl.BlockSpec(memory_space=pltpu.SMEM)


ANY = pl.BlockSpec(memory_space=pl.ANY)


def call(body, outs, specs, flops, nbytes, limit, scratch=()):
    return pl.pallas_call(
        body,
        out_shape=outs,
        in_specs=specs,
        out_specs=[VMEM] * len(outs),
        scratch_shapes=scratch,
        compiler_params=pltpu.CompilerParams(vmem_limit_bytes=limit * MIB),
        cost_estimate=pl.CostEstimate(flops=flops, bytes_accessed=nbytes, transcendentals=0),
    )


def bf16(shape):
    return jax.ShapeDtypeStruct(shape, jnp.bfloat16)


def in_hbm(array):
    return pltpu.with_memory_space_constraint(array, pltpu.HBM)


def slot_tables(owner, routes, shares):
    tokens = routes.shape[1]
    slot = lax.broadcasted_iota(jnp.int32, (EF * CAP, tokens), 0)
    first = slot < CAP
    weights = []
    members = []
    for expert in (owner, 1 - owner):
        hit = routes == expert
        members.append(jnp.sum(jnp.where(hit, 1.0, 0.0), axis=0, keepdims=True))
        weights.append(jnp.sum(jnp.where(hit, shares, 0.0), axis=0, keepdims=True))
    member = jnp.where(first, members[0], members[1])
    row = lax.broadcasted_iota(jnp.int32, (tokens, tokens), 0)
    col = lax.broadcasted_iota(jnp.int32, (tokens, tokens), 1)
    earlier = jnp.where(row < col, 1.0, 0.0).astype(jnp.bfloat16)
    rank = jnp.dot(member.astype(jnp.bfloat16), earlier, preferred_element_type=jnp.float32)
    place = (slot % CAP).astype(jnp.float32)
    placed = jnp.where((member > 0.5) & (rank == place), 1.0, 0.0)
    return placed, weights


def turned(table):
    rows, tokens = table.shape
    return jnp.transpose(jnp.concatenate([table, jnp.zeros((LANES - rows, tokens), jnp.float32)], axis=0))


def started(pairs, sem):
    loads = [pltpu.make_async_copy(src, dst, sem.at[i]) for i, (src, dst) in enumerate(pairs)]
    for load in loads:
        load.start()
    return loads


def dispatch(owner_ref, *refs):
    loads = started(list(zip(refs[:7], refs[11:18])), refs[18])
    own_ref, other_ref, forward_ref, backward_ref = refs[7:11]
    routes_f, shares_f, routes_b, shares_b, rows_f, rows_b, grads = refs[11:18]
    owner = owner_ref[0]
    for load in loads[:4]:
        load.wait()
    placed, weights = slot_tables(owner, routes_f[0], shares_f[0])
    pieces = []
    for weight in weights:
        left = weight
        for _ in range(3):
            part = left.astype(jnp.bfloat16).astype(jnp.float32)
            left = left - part
            pieces.append(part)
    pieces.append(jnp.zeros((2, placed.shape[1]), jnp.float32))
    table = jnp.concatenate([placed, *pieces], axis=0)
    forward_ref[...] = turned(table).astype(jnp.bfloat16)
    pick = placed.astype(jnp.bfloat16)
    loads[4].wait()
    slots = jnp.dot(pick, rows_f[0], preferred_element_type=jnp.float32)
    own_ref[:CAP] = slots[:CAP].astype(jnp.bfloat16)
    other_ref[:CAP] = slots[CAP:].astype(jnp.bfloat16)

    placed, weights = slot_tables(owner, routes_b[0], shares_b[0])
    backward_ref[...] = turned(placed).astype(jnp.bfloat16)
    slot = lax.broadcasted_iota(jnp.int32, placed.shape, 0)
    share = placed * jnp.where(slot < CAP, weights[0], weights[1])
    share = jnp.sum(share, axis=1, keepdims=True)
    pick = placed.astype(jnp.bfloat16)
    loads[5].wait()
    slots = jnp.dot(pick, rows_b[0], preferred_element_type=jnp.float32)
    own_ref[CAP : 2 * CAP] = slots[:CAP].astype(jnp.bfloat16)
    other_ref[CAP : 2 * CAP] = slots[CAP:].astype(jnp.bfloat16)
    loads[6].wait()
    slots = share * jnp.dot(pick, grads[0], preferred_element_type=jnp.float32)
    own_ref[2 * CAP :] = slots[:CAP].astype(jnp.bfloat16)
    other_ref[2 * CAP :] = slots[CAP:].astype(jnp.bfloat16)


def load(*refs):
    rows_f, rows_b, table_f, table_b = refs[3:7]
    early_f, early_b, sem = refs[10:]
    width = rows_f.shape[2]
    pairs = [(rows_f.at[0], early_f.at[:, :width]), (rows_b.at[0], early_b.at[:, :width])]
    loads = started(pairs + list(zip(refs[:3], refs[7:10])), sem)
    early_f[:, width:] = table_f[...]
    early_b[:, width:] = table_b[...]
    for each in loads:
        each.wait()


def project(left, right):
    return lax.dot_general(
        left, right, (((1,), (1,)), ((), ())), preferred_element_type=jnp.float32
    )


def unit_rows(rows):
    values = rows.astype(jnp.float32)
    scale = lax.rsqrt(jnp.mean(values * values, axis=-1, keepdims=True) + EPSILON)
    return values * scale, scale


def halving(blocks):
    bits = blocks.bit_length() - 1
    return sorted(range(blocks), key=lambda k: [k >> b & 1 for b in range(bits)])


def give(outs, rows):
    order = halving(rows.shape[0] // CAP)
    rows = jnp.concatenate([rows[k * CAP : (k + 1) * CAP] for k in order], axis=0)
    split = rows.shape[0] // 2
    outs[0][...] = rows[:split]
    outs[1][...] = rows[split:]


def add_received(kept_ref, received_ref, *outs):
    total = kept_ref[...].astype(jnp.float32) + received_ref[...].astype(jnp.float32)
    total = total.astype(jnp.bfloat16)
    split = total.shape[0] // 2
    outs[0][...] = total[:split]
    outs[1][...] = total[split:]


def expert_forward(blocks, *refs):
    rows = jnp.concatenate([ref[:CAP] for ref in refs[:blocks]], axis=0)
    gain_ref, gate_ref, up_ref, down_ref = refs[blocks : blocks + 4]
    outs = refs[blocks + 4 :]
    unit, _ = unit_rows(rows)
    normed = (unit * gain_ref[...]).astype(jnp.bfloat16)
    gate = project(normed, gate_ref[0])
    upper = project(normed, up_ref[0])
    hidden = (gate * jax.nn.sigmoid(gate) * upper).astype(jnp.bfloat16)
    result = jnp.dot(hidden, down_ref[0], preferred_element_type=jnp.float32)
    result = result.astype(jnp.bfloat16)
    give(outs, result)


def expert_backward(blocks, *refs):
    gain_ref, gate_ref, up_ref, down_ref = refs[blocks : blocks + 4]
    outs = refs[blocks + 4 :]
    rows = jnp.concatenate([ref[CAP : 2 * CAP] for ref in refs[:blocks]], axis=0)
    grads = jnp.concatenate([ref[2 * CAP :] for ref in refs[:blocks]], axis=0)
    gain = gain_ref[...]
    unit, scale = unit_rows(rows)
    normed = (unit * gain).astype(jnp.bfloat16)
    hidden_grad = project(grads, down_ref[0])
    gate = project(normed, gate_ref[0])
    upper = project(normed, up_ref[0])
    sigma = jax.nn.sigmoid(gate)
    gate_grad = (hidden_grad * upper * sigma * (1.0 + gate * (1.0 - sigma))).astype(jnp.bfloat16)
    upper_grad = (hidden_grad * gate * sigma).astype(jnp.bfloat16)
    total = jnp.dot(gate_grad, gate_ref[0], preferred_element_type=jnp.float32)
    total = total + jnp.dot(upper_grad, up_ref[0], preferred_element_type=jnp.float32)
    scaled = total * gain
    inner = jnp.mean(scaled * unit, axis=-1, keepdims=True)
    result = (scale * (scaled - unit * inner)).astype(jnp.bfloat16)
    give(outs, result)


def combine_forward(early_ref, own_ref, other_ref, out_ref):
    width = out_ref.shape[2]
    total = early_ref[:, :width].astype(jnp.float32)
    table = early_ref[:, width:]
    for e, part_ref in enumerate((own_ref, other_ref)):
        pick = table[:, e * CAP : (e + 1) * CAP]
        column = EF * CAP + 3 * e
        weight = jnp.sum(
            table[:, column : column + 3].astype(jnp.float32), axis=1, keepdims=True
        )
        total = total + weight * jnp.dot(pick, part_ref[...], preferred_element_type=jnp.float32)
    out_ref[0] = total.astype(jnp.bfloat16)


def combine_backward(early_ref, own_ref, other_ref, out_ref):
    width = out_ref.shape[2]
    pick = early_ref[:, width : width + EF * CAP]
    parts = jnp.concatenate([own_ref[...], other_ref[...]], axis=0)
    total = early_ref[:, :width].astype(jnp.float32)
    total = total + jnp.dot(pick, parts, preferred_element_type=jnp.float32)
    out_ref[0] = total.astype(jnp.bfloat16)


def on_device(
    sections,
    devices,
    forward_input,
    forward_routes,
    forward_shares,
    backward_input,
    backward_routes,
    backward_shares,
    output_grad,
    norm_gain,
    gate_weight,
    up_weight,
    down_weight,
):
    half = devices // EF
    tokens, width = forward_input.shape[1:]
    hidden = gate_weight.shape[1]
    owner = (lax.axis_index("expert") // half).astype(jnp.int32)[None]

    def swapped(block, k):
        return lax.ppermute(block, "expert", [(i, i ^ k) for i in range(devices)])

    def moved(block, distance):
        route = [(i, (i + distance) % sections) for i in range(sections)]
        return lax.ppermute(block, "section", route)

    def returned(block, distance, k):
        route = [
            (s * devices + z, (s + distance) % sections * devices + (z ^ k))
            for s in range(sections)
            for z in range(devices)
        ]
        return lax.ppermute(block, ("section", "expert"), route)

    def gathered(own, other, held):
        blocks = [own]
        far = [swapped(other, half)]
        step = 1
        while step < half:
            blocks = blocks + [swapped(b, step) for b in blocks]
            far, blocks, *held = lax.optimization_barrier((far, blocks, *held))
            far = far + [swapped(b, step) for b in far]
            step *= 2
        return blocks + far, held

    dispatch_bytes = 3 * tokens * width * 2
    lists = forward_routes.shape[:0:-1]
    groups = (forward_routes, forward_shares, backward_routes, backward_shares)
    layers = (forward_input, backward_input, output_grad)
    own, other, table_f, table_b = call(
        dispatch,
        [bf16((3 * CAP, width))] * 2 + [bf16((tokens, LANES))] * 2,
        [SMEM] + [ANY] * 7,
        6 * EF * CAP * tokens * width,
        dispatch_bytes,
        24,
        [pltpu.VMEM((1, *lists), a.dtype) for a in groups]
        + [pltpu.VMEM((1, tokens, width), jnp.bfloat16)] * 3
        + [pltpu.SemaphoreType.DMA((7,))],
    )(owner, *(in_hbm(jnp.swapaxes(a, 1, 2)) for a in groups), *(in_hbm(a) for a in layers))

    weights = (gate_weight, up_weight, down_weight)
    *held, early_f, early_b = call(
        load,
        [pltpu.VMEM(w.shape, w.dtype) for w in weights] + [bf16((tokens, width + LANES))] * 2,
        [ANY] * 5 + [VMEM] * 2,
        0,
        6 * hidden * width * 2,
        8,
        [pltpu.SemaphoreType.DMA((5,))],
    )(*(in_hbm(w) for w in weights), in_hbm(forward_input), in_hbm(output_grad), table_f, table_b)
    early_b = moved(early_b, -1)
    early_f = moved(early_f, 1)
    blocks, held = gathered(own, other, held)

    rows = devices * CAP
    weight_bytes = 3 * hidden * width * 2
    outs = [bf16((rows // 2, width))] * 2
    parts_f = call(
        functools.partial(expert_forward, devices),
        outs,
        [VMEM] * (devices + 4),
        6 * rows * hidden * width,
        weight_bytes,
        24,
    )(*blocks, norm_gain, *held)
    parts_b = call(
        functools.partial(expert_backward, devices),
        outs,
        [VMEM] * (devices + 4),
        10 * rows * hidden * width,
        weight_bytes,
        24,
    )(*blocks, norm_gain, *held)

    def handed_back(kept, given, distance):
        step = 1
        while step < half:
            quarter = kept.shape[0] // 2
            kept, given = call(
                add_received,
                [bf16((quarter, width))] * 2,
                [VMEM] * 2,
                0,
                6 * kept.shape[0] * width,
                8,
            )(kept, swapped(given, step))
            step *= 2
        return returned(kept, distance, 0), returned(given, distance, half)

    parts_f = handed_back(*parts_f, 1)
    parts_b = handed_back(*parts_b, -1)
    result = [bf16((1, tokens, width))]
    combine_flops = 2 * tokens * EF * CAP * width
    (next_input,) = call(
        combine_forward, result, [VMEM] * 3, combine_flops, dispatch_bytes, 24
    )(early_f, *parts_f)
    (previous_gradient,) = call(
        combine_backward, result, [VMEM] * 3, combine_flops, dispatch_bytes, 24
    )(early_b, *parts_b)
    return next_input, previous_gradient


def solution(mesh):
    rows = P("section", "expert", None)
    return jax.shard_map(
        functools.partial(on_device, mesh.shape["section"], mesh.shape["expert"]),
        mesh=mesh,
        in_specs=(rows,) * 7 + (P("section", None),) + (rows,) * 3,
        out_specs=(rows, rows),
        check_vma=False,
    )
```

```python
import functools

import jax
import jax.numpy as jnp
from jax import lax
from jax.experimental import pallas as pl
from jax.experimental.pallas import tpu as pltpu
from jax.sharding import PartitionSpec as P

EF = 2
CAP = 16
EPSILON = 1e-06
LANES = 128
MIB = 1 << 20

VMEM = pl.BlockSpec(memory_space=pltpu.VMEM)
SMEM = pl.BlockSpec(memory_space=pltpu.SMEM)


ANY = pl.BlockSpec(memory_space=pl.ANY)


def call(body, outs, specs, flops, nbytes, limit, scratch=()):
    return pl.pallas_call(
        body,
        out_shape=outs,
        in_specs=specs,
        out_specs=[VMEM] * len(outs),
        scratch_shapes=scratch,
        compiler_params=pltpu.CompilerParams(vmem_limit_bytes=limit * MIB),
        cost_estimate=pl.CostEstimate(flops=flops, bytes_accessed=nbytes, transcendentals=0),
    )


def bf16(shape):
    return jax.ShapeDtypeStruct(shape, jnp.bfloat16)


def in_hbm(array):
    return pltpu.with_memory_space_constraint(array, pltpu.HBM)


def slot_tables(owner, routes, shares):
    tokens = routes.shape[1]
    slot = lax.broadcasted_iota(jnp.int32, (EF * CAP, tokens), 0)
    first = slot < CAP
    weights = []
    members = []
    for expert in (owner, 1 - owner):
        hit = routes == expert
        members.append(jnp.sum(jnp.where(hit, 1.0, 0.0), axis=0, keepdims=True))
        weights.append(jnp.sum(jnp.where(hit, shares, 0.0), axis=0, keepdims=True))
    member = jnp.where(first, members[0], members[1])
    row = lax.broadcasted_iota(jnp.int32, (tokens, tokens), 0)
    col = lax.broadcasted_iota(jnp.int32, (tokens, tokens), 1)
    earlier = jnp.where(row < col, 1.0, 0.0).astype(jnp.bfloat16)
    rank = jnp.dot(member.astype(jnp.bfloat16), earlier, preferred_element_type=jnp.float32)
    place = (slot % CAP).astype(jnp.float32)
    placed = jnp.where((member > 0.5) & (rank == place), 1.0, 0.0)
    return placed, weights


def turned(table):
    rows, tokens = table.shape
    return jnp.transpose(jnp.concatenate([table, jnp.zeros((LANES - rows, tokens), jnp.float32)], axis=0))


def started(pairs, sem):
    loads = [pltpu.make_async_copy(src, dst, sem.at[i]) for i, (src, dst) in enumerate(pairs)]
    for load in loads:
        load.start()
    return loads


def dispatch(owner_ref, *refs):
    loads = started(list(zip(refs[:7], refs[11:18])), refs[18])
    own_ref, other_ref, forward_ref, backward_ref = refs[7:11]
    routes_f, shares_f, routes_b, shares_b, rows_f, rows_b, grads = refs[11:18]
    owner = owner_ref[0]
    for load in loads[:4]:
        load.wait()
    placed, weights = slot_tables(owner, routes_f[0], shares_f[0])
    pieces = []
    for weight in weights:
        left = weight
        for _ in range(3):
            part = left.astype(jnp.bfloat16).astype(jnp.float32)
            left = left - part
            pieces.append(part)
    pieces.append(jnp.zeros((2, placed.shape[1]), jnp.float32))
    table = jnp.concatenate([placed, *pieces], axis=0)
    forward_ref[...] = turned(table).astype(jnp.bfloat16)
    pick = placed.astype(jnp.bfloat16)
    loads[4].wait()
    slots = jnp.dot(pick, rows_f[0], preferred_element_type=jnp.float32)
    own_ref[:CAP] = slots[:CAP].astype(jnp.bfloat16)
    other_ref[:CAP] = slots[CAP:].astype(jnp.bfloat16)

    placed, weights = slot_tables(owner, routes_b[0], shares_b[0])
    backward_ref[...] = turned(placed).astype(jnp.bfloat16)
    slot = lax.broadcasted_iota(jnp.int32, placed.shape, 0)
    share = placed * jnp.where(slot < CAP, weights[0], weights[1])
    share = jnp.sum(share, axis=1, keepdims=True)
    pick = placed.astype(jnp.bfloat16)
    loads[5].wait()
    slots = jnp.dot(pick, rows_b[0], preferred_element_type=jnp.float32)
    own_ref[CAP : 2 * CAP] = slots[:CAP].astype(jnp.bfloat16)
    other_ref[CAP : 2 * CAP] = slots[CAP:].astype(jnp.bfloat16)
    loads[6].wait()
    slots = share * jnp.dot(pick, grads[0], preferred_element_type=jnp.float32)
    own_ref[2 * CAP :] = slots[:CAP].astype(jnp.bfloat16)
    other_ref[2 * CAP :] = slots[CAP:].astype(jnp.bfloat16)


def load(pieces, rows_f, rows_b, table_f, table_b, *refs):
    *refs, early_sem, sem = refs
    count = (len(refs) - 2) // 3
    early_f, early_b = refs[count : count + 2]
    source, held, turned_ref = refs[:count], refs[count + 2 : -count], refs[-count:]
    width = rows_f.shape[2]
    size = held[0].shape[1] // pieces
    spans = [pl.ds(piece * size, size) for piece in range(pieces)]
    pairs = [(src.at[0, span], dst.at[0, span]) for span in spans for src, dst in zip(source, held)]
    loads = started(pairs, sem)
    early = started(
        [(rows_f.at[0], early_f.at[:, :width]), (rows_b.at[0], early_b.at[:, :width])], early_sem
    )
    early_f[:, width:] = table_f[...]
    early_b[:, width:] = table_b[...]
    for piece, span in enumerate(spans):
        for i in range(count):
            loads[piece * count + i].wait()
            turned_ref[i][:, span] = held[i][0, span].T
    for each in early:
        each.wait()


def product(left, right_ref):
    return jnp.dot(left, right_ref[...], preferred_element_type=jnp.float32)


def unit_rows(rows):
    values = rows.astype(jnp.float32)
    scale = lax.rsqrt(jnp.mean(values * values, axis=-1, keepdims=True) + EPSILON)
    return values * scale, scale


def halving(blocks):
    bits = blocks.bit_length() - 1
    return sorted(range(blocks), key=lambda k: [k >> b & 1 for b in range(bits)])


def give(outs, rows):
    order = halving(rows.shape[0] // CAP)
    rows = jnp.concatenate([rows[k * CAP : (k + 1) * CAP] for k in order], axis=0)
    split = rows.shape[0] // 2
    outs[0][...] = rows[:split]
    outs[1][...] = rows[split:]


def add_received(kept_ref, received_ref, *outs):
    total = kept_ref[...].astype(jnp.float32) + received_ref[...].astype(jnp.float32)
    total = total.astype(jnp.bfloat16)
    split = total.shape[0] // 2
    outs[0][...] = total[:split]
    outs[1][...] = total[split:]


def expert_forward(blocks, *refs):
    gain_ref, gate_turned, up_turned, down_ref = refs[blocks : blocks + 4]
    kept_ref, given_ref, to_gate_ref, to_up_ref = refs[blocks + 4 :]
    rows = [ref[:CAP] for ref in refs[:blocks]] + [ref[CAP : 2 * CAP] for ref in refs[:blocks]]
    unit, _ = unit_rows(jnp.concatenate(rows, axis=0))
    normed = (unit * gain_ref[...]).astype(jnp.bfloat16)
    gate = product(normed, gate_turned)
    upper = product(normed, up_turned)
    split = blocks * CAP
    sigma = jax.nn.sigmoid(gate)
    passed = gate * sigma
    hidden = (passed[:split] * upper[:split]).astype(jnp.bfloat16)
    to_up_ref[...] = passed[split:]
    to_gate_ref[...] = (upper * sigma * (1.0 + gate * (1.0 - sigma)))[split:]
    give((kept_ref, given_ref), product(hidden, down_ref.at[0]).astype(jnp.bfloat16))


def expert_backward(blocks, *refs):
    gain_ref, to_gate_ref, to_up_ref, gate_ref, up_ref, down_turned = refs[blocks : blocks + 6]
    grads = jnp.concatenate([ref[2 * CAP :] for ref in refs[:blocks]], axis=0)
    hidden_grad = product(grads, down_turned)
    gate_grad = (hidden_grad * to_gate_ref[...]).astype(jnp.bfloat16)
    upper_grad = (hidden_grad * to_up_ref[...]).astype(jnp.bfloat16)
    total = product(gate_grad, gate_ref.at[0]) + product(upper_grad, up_ref.at[0])
    rows = jnp.concatenate([ref[CAP : 2 * CAP] for ref in refs[:blocks]], axis=0)
    unit, scale = unit_rows(rows)
    scaled = total * gain_ref[...]
    inner = jnp.mean(scaled * unit, axis=-1, keepdims=True)
    give(refs[blocks + 6 :], (scale * (scaled - unit * inner)).astype(jnp.bfloat16))


def combine_forward(early_ref, own_ref, other_ref, out_ref):
    width = out_ref.shape[2]
    total = early_ref[:, :width].astype(jnp.float32)
    table = early_ref[:, width:]
    for e, part_ref in enumerate((own_ref, other_ref)):
        pick = table[:, e * CAP : (e + 1) * CAP]
        column = EF * CAP + 3 * e
        weight = jnp.sum(
            table[:, column : column + 3].astype(jnp.float32), axis=1, keepdims=True
        )
        total = total + weight * jnp.dot(pick, part_ref[...], preferred_element_type=jnp.float32)
    out_ref[0] = total.astype(jnp.bfloat16)


def combine_backward(early_ref, own_ref, other_ref, out_ref):
    width = out_ref.shape[2]
    pick = early_ref[:, width : width + EF * CAP]
    parts = jnp.concatenate([own_ref[...], other_ref[...]], axis=0)
    total = early_ref[:, :width].astype(jnp.float32)
    total = total + jnp.dot(pick, parts, preferred_element_type=jnp.float32)
    out_ref[0] = total.astype(jnp.bfloat16)


def on_device(
    sections,
    devices,
    forward_input,
    forward_routes,
    forward_shares,
    backward_input,
    backward_routes,
    backward_shares,
    output_grad,
    norm_gain,
    gate_weight,
    up_weight,
    down_weight,
):
    half = devices // EF
    tokens, width = forward_input.shape[1:]
    hidden = gate_weight.shape[1]
    owner = (lax.axis_index("expert") // half).astype(jnp.int32)[None]

    def swapped(block, k):
        return lax.ppermute(block, "expert", [(i, i ^ k) for i in range(devices)])

    def moved(block, distance):
        route = [(i, (i + distance) % sections) for i in range(sections)]
        return lax.ppermute(block, "section", route)

    def returned(block, distance, k):
        route = [
            (s * devices + z, (s + distance) % sections * devices + (z ^ k))
            for s in range(sections)
            for z in range(devices)
        ]
        return lax.ppermute(block, ("section", "expert"), route)

    def gathered(own, other, held):
        blocks = [own]
        far = [swapped(other, half)]
        step = 1
        while step < half:
            blocks = blocks + [swapped(b, step) for b in blocks]
            far, blocks, *held = lax.optimization_barrier((far, blocks, *held))
            far = far + [swapped(b, step) for b in far]
            step *= 2
        return blocks + far, held

    dispatch_bytes = 3 * tokens * width * 2
    lists = forward_routes.shape[:0:-1]
    groups = (forward_routes, forward_shares, backward_routes, backward_shares)
    layers = (forward_input, backward_input, output_grad)
    own, other, table_f, table_b = call(
        dispatch,
        [bf16((3 * CAP, width))] * 2 + [bf16((tokens, LANES))] * 2,
        [SMEM] + [ANY] * 7,
        6 * EF * CAP * tokens * width,
        dispatch_bytes,
        24,
        [pltpu.VMEM((1, *lists), a.dtype) for a in groups]
        + [pltpu.VMEM((1, tokens, width), jnp.bfloat16)] * 3
        + [pltpu.SemaphoreType.DMA((7,))],
    )(owner, *(in_hbm(jnp.swapaxes(a, 1, 2)) for a in groups), *(in_hbm(a) for a in layers))

    weights = (gate_weight, up_weight, down_weight)
    pieces = 3 if hidden % (3 * LANES) == 0 else 1
    early_f, early_b, *held = call(
        functools.partial(load, pieces),
        [bf16((tokens, width + LANES))] * 2
        + [pltpu.VMEM(w.shape, w.dtype) for w in weights]
        + [pltpu.VMEM((width, hidden), w.dtype) for w in weights],
        [ANY] * 2 + [VMEM] * 2 + [ANY] * 3,
        0,
        12 * hidden * width * 2,
        8,
        [pltpu.SemaphoreType.DMA((2,)), pltpu.SemaphoreType.DMA((3 * pieces,))],
    )(
        in_hbm(forward_input),
        in_hbm(output_grad),
        table_f,
        table_b,
        *(in_hbm(w) for w in weights),
    )
    early_b = moved(early_b, -1)
    early_f = moved(early_f, 1)
    blocks, held = gathered(own, other, held)
    gate, up, down, gate_turned, up_turned, down_turned = held

    rows = devices * CAP
    weight_bytes = 3 * hidden * width * 2
    outs = [bf16((rows // 2, width))] * 2
    factor = jax.ShapeDtypeStruct((rows, hidden), jnp.float32)
    *parts_f, to_gate, to_up = call(
        functools.partial(expert_forward, devices),
        outs + [factor] * 2,
        [VMEM] * (devices + 4),
        10 * rows * hidden * width,
        weight_bytes,
        16,
    )(*blocks, norm_gain, gate_turned, up_turned, down)
    parts_b = call(
        functools.partial(expert_backward, devices),
        outs,
        [VMEM] * (devices + 6),
        6 * rows * hidden * width,
        weight_bytes,
        16,
    )(*blocks, norm_gain, to_gate, to_up, gate, up, down_turned)

    def handed_back(kept, given, distance):
        step = 1
        while step < half:
            quarter = kept.shape[0] // 2
            kept, given = call(
                add_received,
                [bf16((quarter, width))] * 2,
                [VMEM] * 2,
                0,
                6 * kept.shape[0] * width,
                8,
            )(kept, swapped(given, step))
            step *= 2
        return returned(kept, distance, 0), returned(given, distance, half)

    parts_f = handed_back(*parts_f, 1)
    parts_b = handed_back(*parts_b, -1)
    result = [bf16((1, tokens, width))]
    combine_flops = 2 * tokens * EF * CAP * width
    (next_input,) = call(
        combine_forward, result, [VMEM] * 3, combine_flops, dispatch_bytes, 24
    )(early_f, *parts_f)
    (previous_gradient,) = call(
        combine_backward, result, [VMEM] * 3, combine_flops, dispatch_bytes, 24
    )(early_b, *parts_b)
    return next_input, previous_gradient


def solution(mesh):
    rows = P("section", "expert", None)
    return jax.shard_map(
        functools.partial(on_device, mesh.shape["section"], mesh.shape["expert"]),
        mesh=mesh,
        in_specs=(rows,) * 7 + (P("section", None),) + (rows,) * 3,
        out_specs=(rows, rows),
        check_vma=False,
    )
```

```python
import functools

import jax
import jax.numpy as jnp
from jax import lax
from jax.experimental import pallas as pl
from jax.experimental.pallas import tpu as pltpu
from jax.sharding import PartitionSpec as P

EF = 2
CAP = 16
EPSILON = 1e-06
OUT_PIECES = 4
LANES = 128
MIB = 1 << 20

VMEM = pl.BlockSpec(memory_space=pltpu.VMEM)
SMEM = pl.BlockSpec(memory_space=pltpu.SMEM)


ANY = pl.BlockSpec(memory_space=pl.ANY)


def call(body, outs, specs, flops, nbytes, limit, scratch=(), out_spec=VMEM):
    return pl.pallas_call(
        body,
        out_shape=outs,
        in_specs=specs,
        out_specs=[out_spec] * len(outs),
        scratch_shapes=scratch,
        compiler_params=pltpu.CompilerParams(vmem_limit_bytes=limit * MIB),
        cost_estimate=pl.CostEstimate(flops=flops, bytes_accessed=nbytes, transcendentals=0),
    )


def bf16(shape):
    return jax.ShapeDtypeStruct(shape, jnp.bfloat16)


def in_hbm(array):
    return pltpu.with_memory_space_constraint(array, pltpu.HBM)


def slot_tables(owner, routes, shares):
    tokens = routes.shape[1]
    slot = lax.broadcasted_iota(jnp.int32, (EF * CAP, tokens), 0)
    first = slot < CAP
    weights = []
    members = []
    for expert in (owner, 1 - owner):
        hit = routes == expert
        members.append(jnp.sum(jnp.where(hit, 1.0, 0.0), axis=0, keepdims=True))
        weights.append(jnp.sum(jnp.where(hit, shares, 0.0), axis=0, keepdims=True))
    member = jnp.where(first, members[0], members[1])
    row = lax.broadcasted_iota(jnp.int32, (tokens, tokens), 0)
    col = lax.broadcasted_iota(jnp.int32, (tokens, tokens), 1)
    earlier = jnp.where(row < col, 1.0, 0.0).astype(jnp.bfloat16)
    rank = jnp.dot(member.astype(jnp.bfloat16), earlier, preferred_element_type=jnp.float32)
    place = (slot % CAP).astype(jnp.float32)
    placed = jnp.where((member > 0.5) & (rank == place), 1.0, 0.0)
    return placed, weights


def turned(table):
    rows, tokens = table.shape
    return jnp.transpose(jnp.concatenate([table, jnp.zeros((LANES - rows, tokens), jnp.float32)], axis=0))


def started(pairs, sem):
    loads = [pltpu.make_async_copy(src, dst, sem.at[i]) for i, (src, dst) in enumerate(pairs)]
    for load in loads:
        load.start()
    return loads


def dispatch(owner_ref, *refs):
    loads = started(list(zip(refs[:7], refs[11:18])), refs[18])
    own_ref, other_ref, forward_ref, backward_ref = refs[7:11]
    routes_f, shares_f, routes_b, shares_b, rows_f, rows_b, grads = refs[11:18]
    owner = owner_ref[0]
    for load in loads[:4]:
        load.wait()
    placed, weights = slot_tables(owner, routes_f[0], shares_f[0])
    pieces = []
    for weight in weights:
        left = weight
        for _ in range(3):
            part = left.astype(jnp.bfloat16).astype(jnp.float32)
            left = left - part
            pieces.append(part)
    pieces.append(jnp.zeros((2, placed.shape[1]), jnp.float32))
    table = jnp.concatenate([placed, *pieces], axis=0)
    forward_ref[...] = turned(table).astype(jnp.bfloat16)
    pick = placed.astype(jnp.bfloat16)
    loads[4].wait()
    slots = jnp.dot(pick, rows_f[0], preferred_element_type=jnp.float32)
    own_ref[:CAP] = slots[:CAP].astype(jnp.bfloat16)
    other_ref[:CAP] = slots[CAP:].astype(jnp.bfloat16)

    placed, weights = slot_tables(owner, routes_b[0], shares_b[0])
    backward_ref[...] = turned(placed).astype(jnp.bfloat16)
    slot = lax.broadcasted_iota(jnp.int32, placed.shape, 0)
    share = placed * jnp.where(slot < CAP, weights[0], weights[1])
    share = jnp.sum(share, axis=1, keepdims=True)
    pick = placed.astype(jnp.bfloat16)
    loads[5].wait()
    slots = jnp.dot(pick, rows_b[0], preferred_element_type=jnp.float32)
    own_ref[CAP : 2 * CAP] = slots[:CAP].astype(jnp.bfloat16)
    other_ref[CAP : 2 * CAP] = slots[CAP:].astype(jnp.bfloat16)
    loads[6].wait()
    slots = share * jnp.dot(pick, grads[0], preferred_element_type=jnp.float32)
    own_ref[2 * CAP :] = slots[:CAP].astype(jnp.bfloat16)
    other_ref[2 * CAP :] = slots[CAP:].astype(jnp.bfloat16)


def load(pieces, rows_f, rows_b, table_f, table_b, *refs):
    *refs, early_sem, sem = refs
    count = (len(refs) - 2) // 3
    early_f, early_b = refs[count : count + 2]
    source, held, turned_ref = refs[:count], refs[count + 2 : -count], refs[-count:]
    width = rows_f.shape[2]
    size = held[0].shape[1] // pieces
    spans = [pl.ds(piece * size, size) for piece in range(pieces)]
    pairs = [(src.at[0, span], dst.at[0, span]) for span in spans for src, dst in zip(source, held)]
    loads = started(pairs, sem)
    early = started(
        [(rows_f.at[0], early_f.at[:, :width]), (rows_b.at[0], early_b.at[:, :width])], early_sem
    )
    early_f[:, width:] = table_f[...]
    early_b[:, width:] = table_b[...]
    for piece, span in enumerate(spans):
        for i in range(count):
            loads[piece * count + i].wait()
            turned_ref[i][:, span] = held[i][0, span].T
    for each in early:
        each.wait()


def product(left, right_ref):
    return jnp.dot(left, right_ref[...], preferred_element_type=jnp.float32)


def wide_product(left, right_ref):
    rows, depth = left.shape
    if rows >= LANES:
        return product(left, right_ref)
    below = jnp.zeros((LANES - rows, depth), left.dtype)
    return product(jnp.concatenate([left, below], axis=0), right_ref)[:rows]


def unit_rows(rows):
    values = rows.astype(jnp.float32)
    scale = lax.rsqrt(jnp.mean(values * values, axis=-1, keepdims=True) + EPSILON)
    return values * scale, scale


def halving(blocks):
    bits = blocks.bit_length() - 1
    return sorted(range(blocks), key=lambda k: [k >> b & 1 for b in range(bits)])


def give(outs, rows):
    order = halving(rows.shape[0] // CAP)
    rows = jnp.concatenate([rows[k * CAP : (k + 1) * CAP] for k in order], axis=0)
    split = rows.shape[0] // 2
    outs[0][...] = rows[:split]
    outs[1][...] = rows[split:]


def add_received(kept_ref, received_ref, *outs):
    total = kept_ref[...].astype(jnp.float32) + received_ref[...].astype(jnp.float32)
    total = total.astype(jnp.bfloat16)
    split = total.shape[0] // 2
    outs[0][...] = total[:split]
    outs[1][...] = total[split:]


def expert_forward(blocks, *refs):
    gain_ref, gate_turned, up_turned, down_ref = refs[blocks : blocks + 4]
    kept_ref, given_ref, to_gate_ref, to_up_ref = refs[blocks + 4 :]
    rows = [ref[:CAP] for ref in refs[:blocks]] + [ref[CAP : 2 * CAP] for ref in refs[:blocks]]
    unit, _ = unit_rows(jnp.concatenate(rows, axis=0))
    normed = (unit * gain_ref[...]).astype(jnp.bfloat16)
    gate = product(normed, gate_turned)
    upper = product(normed, up_turned)
    split = blocks * CAP
    sigma = jax.nn.sigmoid(gate)
    passed = gate * sigma
    hidden = (passed[:split] * upper[:split]).astype(jnp.bfloat16)
    to_up_ref[...] = passed[split:]
    to_gate_ref[...] = (upper * sigma * (1.0 + gate * (1.0 - sigma)))[split:]
    give((kept_ref, given_ref), product(hidden, down_ref.at[0]).astype(jnp.bfloat16))


def expert_backward(blocks, *refs):
    gain_ref, to_gate_ref, to_up_ref, gate_ref, up_ref, down_turned = refs[blocks : blocks + 6]
    grads = jnp.concatenate([ref[2 * CAP :] for ref in refs[:blocks]], axis=0)
    hidden_grad = wide_product(grads, down_turned)
    gate_grad = (hidden_grad * to_gate_ref[...]).astype(jnp.bfloat16)
    upper_grad = (hidden_grad * to_up_ref[...]).astype(jnp.bfloat16)
    total = wide_product(gate_grad, gate_ref.at[0]) + wide_product(upper_grad, up_ref.at[0])
    rows = jnp.concatenate([ref[CAP : 2 * CAP] for ref in refs[:blocks]], axis=0)
    unit, scale = unit_rows(rows)
    scaled = total * gain_ref[...]
    inner = jnp.mean(scaled * unit, axis=-1, keepdims=True)
    give(refs[blocks + 6 :], (scale * (scaled - unit * inner)).astype(jnp.bfloat16))


def sent_out(out_hbm, held_ref, sem, columns):
    width = held_ref.shape[1]
    size = width // OUT_PIECES
    copies = []
    for piece in range(OUT_PIECES):
        span = pl.ds(piece * size, size)
        held_ref[:, span] = columns(span).astype(jnp.bfloat16)
        copy = pltpu.make_async_copy(
            held_ref.at[:, span], out_hbm.at[0, :, span], sem.at[piece]
        )
        copy.start()
        copies.append(copy)
    for copy in copies:
        copy.wait()


def combine_forward(early_ref, own_ref, other_ref, out_hbm, held_ref, sem):
    table = early_ref[:, held_ref.shape[1] :]
    picks = []
    for e in range(EF):
        column = EF * CAP + 3 * e
        weight = jnp.sum(
            table[:, column : column + 3].astype(jnp.float32), axis=1, keepdims=True
        )
        picks.append((table[:, e * CAP : (e + 1) * CAP], weight))

    def columns(span):
        total = early_ref[:, span].astype(jnp.float32)
        for (pick, weight), part_ref in zip(picks, (own_ref, other_ref)):
            total = total + weight * product(pick, part_ref.at[:, span])
        return total

    sent_out(out_hbm, held_ref, sem, columns)


def combine_backward(early_ref, own_ref, other_ref, out_hbm, held_ref, sem):
    width = held_ref.shape[1]
    pick = early_ref[:, width : width + EF * CAP]

    def columns(span):
        parts = jnp.concatenate([own_ref[:, span], other_ref[:, span]], axis=0)
        total = jnp.dot(pick, parts, preferred_element_type=jnp.float32)
        return early_ref[:, span].astype(jnp.float32) + total

    sent_out(out_hbm, held_ref, sem, columns)


def on_device(
    sections,
    devices,
    forward_input,
    forward_routes,
    forward_shares,
    backward_input,
    backward_routes,
    backward_shares,
    output_grad,
    norm_gain,
    gate_weight,
    up_weight,
    down_weight,
):
    half = devices // EF
    tokens, width = forward_input.shape[1:]
    hidden = gate_weight.shape[1]
    owner = (lax.axis_index("expert") // half).astype(jnp.int32)[None]

    def swapped(block, k):
        return lax.ppermute(block, "expert", [(i, i ^ k) for i in range(devices)])

    def moved(block, distance):
        route = [(i, (i + distance) % sections) for i in range(sections)]
        return lax.ppermute(block, "section", route)

    def returned(block, distance, k):
        route = [
            (s * devices + z, (s + distance) % sections * devices + (z ^ k))
            for s in range(sections)
            for z in range(devices)
        ]
        return lax.ppermute(block, ("section", "expert"), route)

    def gathered(own, other, held):
        blocks = [own]
        far = [swapped(other, half)]
        step = 1
        while step < half:
            blocks = blocks + [swapped(b, step) for b in blocks]
            far, blocks, *held = lax.optimization_barrier((far, blocks, *held))
            far = far + [swapped(b, step) for b in far]
            step *= 2
        return blocks + far, held

    dispatch_bytes = 3 * tokens * width * 2
    lists = forward_routes.shape[:0:-1]
    groups = (forward_routes, forward_shares, backward_routes, backward_shares)
    layers = (forward_input, backward_input, output_grad)
    own, other, table_f, table_b = call(
        dispatch,
        [bf16((3 * CAP, width))] * 2 + [bf16((tokens, LANES))] * 2,
        [SMEM] + [ANY] * 7,
        6 * EF * CAP * tokens * width,
        dispatch_bytes,
        24,
        [pltpu.VMEM((1, *lists), a.dtype) for a in groups]
        + [pltpu.VMEM((1, tokens, width), jnp.bfloat16)] * 3
        + [pltpu.SemaphoreType.DMA((7,))],
    )(owner, *(in_hbm(jnp.swapaxes(a, 1, 2)) for a in groups), *(in_hbm(a) for a in layers))

    weights = (gate_weight, up_weight, down_weight)
    pieces = 3 if hidden % (3 * LANES) == 0 else 1
    early_f, early_b, *held = call(
        functools.partial(load, pieces),
        [bf16((tokens, width + LANES))] * 2
        + [pltpu.VMEM(w.shape, w.dtype) for w in weights]
        + [pltpu.VMEM((width, hidden), w.dtype) for w in weights],
        [ANY] * 2 + [VMEM] * 2 + [ANY] * 3,
        0,
        12 * hidden * width * 2,
        8,
        [pltpu.SemaphoreType.DMA((2,)), pltpu.SemaphoreType.DMA((3 * pieces,))],
    )(
        in_hbm(forward_input),
        in_hbm(output_grad),
        table_f,
        table_b,
        *(in_hbm(w) for w in weights),
    )
    early_b = moved(early_b, -1)
    early_f = moved(early_f, 1)
    blocks, held = gathered(own, other, held)
    gate, up, down, gate_turned, up_turned, down_turned = held

    rows = devices * CAP
    weight_bytes = 3 * hidden * width * 2
    outs = [bf16((rows // 2, width))] * 2
    factor = jax.ShapeDtypeStruct((rows, hidden), jnp.float32)
    *parts_f, to_gate, to_up = call(
        functools.partial(expert_forward, devices),
        outs + [factor] * 2,
        [VMEM] * (devices + 4),
        10 * rows * hidden * width,
        weight_bytes,
        16,
    )(*blocks, norm_gain, gate_turned, up_turned, down)
    parts_b = call(
        functools.partial(expert_backward, devices),
        outs,
        [VMEM] * (devices + 6),
        6 * rows * hidden * width,
        weight_bytes,
        16,
    )(*blocks, norm_gain, to_gate, to_up, gate, up, down_turned)

    def handed_back(kept, given, distance):
        step = 1
        while step < half:
            quarter = kept.shape[0] // 2
            kept, given = call(
                add_received,
                [bf16((quarter, width))] * 2,
                [VMEM] * 2,
                0,
                6 * kept.shape[0] * width,
                8,
            )(kept, swapped(given, step))
            step *= 2
        return returned(kept, distance, 0), returned(given, distance, half)

    parts_f = handed_back(*parts_f, 1)
    parts_b = handed_back(*parts_b, -1)
    result = [bf16((1, tokens, width))]
    combine_flops = 2 * tokens * EF * CAP * width
    scratch = [pltpu.VMEM((tokens, width), jnp.bfloat16), pltpu.SemaphoreType.DMA((OUT_PIECES,))]
    (next_input,) = call(
        combine_forward, result, [VMEM] * 3, combine_flops, dispatch_bytes, 16, scratch, ANY
    )(early_f, *parts_f)
    (previous_gradient,) = call(
        combine_backward, result, [VMEM] * 3, combine_flops, dispatch_bytes, 16, scratch, ANY
    )(early_b, *parts_b)
    return next_input, previous_gradient


def solution(mesh):
    rows = P("section", "expert", None)
    return jax.shard_map(
        functools.partial(on_device, mesh.shape["section"], mesh.shape["expert"]),
        mesh=mesh,
        in_specs=(rows,) * 7 + (P("section", None),) + (rows,) * 3,
        out_specs=(rows, rows),
        check_vma=False,
    )
```

```python
import functools

import jax
import jax.numpy as jnp
from jax import lax
from jax.experimental import pallas as pl
from jax.experimental.pallas import tpu as pltpu
from jax.sharding import PartitionSpec as P

EF = 2
CAP = 16
EPSILON = 1e-06
OUT_PIECES = 4
LANES = 128
MIB = 1 << 20

VMEM = pl.BlockSpec(memory_space=pltpu.VMEM)
SMEM = pl.BlockSpec(memory_space=pltpu.SMEM)


ANY = pl.BlockSpec(memory_space=pl.ANY)


def call(body, outs, specs, flops, nbytes, limit, scratch=(), out_spec=VMEM):
    return pl.pallas_call(
        body,
        out_shape=outs,
        in_specs=specs,
        out_specs=[out_spec] * len(outs),
        scratch_shapes=scratch,
        compiler_params=pltpu.CompilerParams(vmem_limit_bytes=limit * MIB),
        cost_estimate=pl.CostEstimate(flops=flops, bytes_accessed=nbytes, transcendentals=0),
    )


def bf16(shape):
    return jax.ShapeDtypeStruct(shape, jnp.bfloat16)


def in_hbm(array):
    return pltpu.with_memory_space_constraint(array, pltpu.HBM)


def slot_tables(owner, groups):
    tokens = groups[0][0].shape[1]
    rows = EF * CAP * len(groups)
    members, weights = [], []
    for routes, shares in groups:
        for expert in (owner, 1 - owner):
            hit = routes == expert
            member = jnp.sum(jnp.where(hit, 1.0, 0.0), axis=0, keepdims=True)
            members.append(jnp.broadcast_to(member, (CAP, tokens)))
            weights.append(jnp.sum(jnp.where(hit, shares, 0.0), axis=0, keepdims=True))
    member = jnp.concatenate(members, axis=0)
    row = lax.broadcasted_iota(jnp.int32, (tokens, tokens), 0)
    col = lax.broadcasted_iota(jnp.int32, (tokens, tokens), 1)
    earlier = jnp.where(row < col, 1.0, 0.0).astype(jnp.bfloat16)
    rank = jnp.dot(member.astype(jnp.bfloat16), earlier, preferred_element_type=jnp.float32)
    place = lax.broadcasted_iota(jnp.int32, (rows, tokens), 0) % CAP
    placed = jnp.where((member > 0.5) & (rank == place.astype(jnp.float32)), 1.0, 0.0)
    return [
        (placed[i * EF * CAP : (i + 1) * EF * CAP], weights[i * EF : (i + 1) * EF])
        for i in range(len(groups))
    ]


def turned(table):
    rows, tokens = table.shape
    return jnp.transpose(jnp.concatenate([table, jnp.zeros((LANES - rows, tokens), jnp.float32)], axis=0))


def started(pairs, sem):
    loads = [pltpu.make_async_copy(src, dst, sem.at[i]) for i, (src, dst) in enumerate(pairs)]
    for load in loads:
        load.start()
    return loads


def dispatch(owner_ref, *refs):
    loads = started(list(zip(refs[:7], refs[11:18])), refs[18])
    own_ref, other_ref, forward_ref, backward_ref = refs[7:11]
    routes_f, shares_f, routes_b, shares_b, rows_f, rows_b, grads = refs[11:18]
    for load in loads[:4]:
        load.wait()
    groups = [(routes_f[0], shares_f[0]), (routes_b[0], shares_b[0])]
    (placed_f, weights_f), (placed_b, weights_b) = slot_tables(owner_ref[0], groups)
    slot = lax.broadcasted_iota(jnp.int32, placed_b.shape, 0)
    share = placed_b * jnp.where(slot < CAP, weights_b[0], weights_b[1])
    share = jnp.sum(share, axis=1, keepdims=True)
    for i, (placed, rows) in enumerate(((placed_f, rows_f), (placed_b, rows_b), (placed_b, grads))):
        loads[4 + i].wait()
        slots = product(placed.astype(jnp.bfloat16), rows.at[0])
        slots = (slots if i < 2 else share * slots).astype(jnp.bfloat16)
        own_ref[i * CAP : (i + 1) * CAP] = slots[:CAP]
        other_ref[i * CAP : (i + 1) * CAP] = slots[CAP:]
    unused = jnp.zeros((8 - EF, placed_f.shape[1]), jnp.float32)
    forward_ref[...] = jnp.concatenate([placed_f, *weights_f, unused], axis=0)
    backward_ref[...] = placed_b


def load(pieces, rows_f, rows_b, table_f, table_b, *refs):
    *refs, early_sem, sem = refs
    count = (len(refs) - 2) // 3
    early_f, early_b = refs[count : count + 2]
    source, held, turned_ref = refs[:count], refs[count + 2 : -count], refs[-count:]
    width = rows_f.shape[2]
    size = held[0].shape[1] // pieces
    spans = [pl.ds(piece * size, size) for piece in range(pieces)]
    pairs = [(src.at[0, span], dst.at[0, span]) for span in spans for src, dst in zip(source, held)]
    loads = started(pairs, sem)
    early = started(
        [(rows_f.at[0], early_f.at[:, :width]), (rows_b.at[0], early_b.at[:, :width])], early_sem
    )
    rows = [table_f[: EF * CAP]]
    for e in range(EF):
        left = table_f[EF * CAP + e : EF * CAP + e + 1]
        for _ in range(3):
            rows.append(left.astype(jnp.bfloat16).astype(jnp.float32))
            left = left - rows[-1]
    rows.append(jnp.zeros((2, left.shape[1]), jnp.float32))
    early_f[:, width:] = turned(jnp.concatenate(rows, axis=0)).astype(jnp.bfloat16)
    early_b[:, width:] = turned(table_b[...]).astype(jnp.bfloat16)
    for piece, span in enumerate(spans):
        for i in range(count):
            loads[piece * count + i].wait()
            turned_ref[i][:, span] = held[i][0, span].T
    for each in early:
        each.wait()


def product(left, right_ref):
    return jnp.dot(left, right_ref[...], preferred_element_type=jnp.float32)


def wide_product(left, right_ref):
    rows, depth = left.shape
    if rows >= LANES:
        return product(left, right_ref)
    below = jnp.zeros((LANES - rows, depth), left.dtype)
    return product(jnp.concatenate([left, below], axis=0), right_ref)[:rows]


def unit_rows(rows):
    values = rows.astype(jnp.float32)
    scale = lax.rsqrt(jnp.mean(values * values, axis=-1, keepdims=True) + EPSILON)
    return values * scale, scale


def halving(blocks):
    bits = blocks.bit_length() - 1
    return sorted(range(blocks), key=lambda k: [k >> b & 1 for b in range(bits)])


def give(outs, rows):
    order = halving(rows.shape[0] // CAP)
    rows = jnp.concatenate([rows[k * CAP : (k + 1) * CAP] for k in order], axis=0)
    split = rows.shape[0] // 2
    outs[0][...] = rows[:split]
    outs[1][...] = rows[split:]


def add_received(kept_ref, received_ref, *outs):
    total = kept_ref[...].astype(jnp.float32) + received_ref[...].astype(jnp.float32)
    total = total.astype(jnp.bfloat16)
    split = total.shape[0] // 2
    outs[0][...] = total[:split]
    outs[1][...] = total[split:]


def expert_forward(blocks, *refs):
    gain_ref, gate_turned, up_turned, down_ref = refs[blocks : blocks + 4]
    kept_ref, given_ref, to_gate_ref, to_up_ref = refs[blocks + 4 :]
    rows = [ref[:CAP] for ref in refs[:blocks]] + [ref[CAP : 2 * CAP] for ref in refs[:blocks]]
    unit, _ = unit_rows(jnp.concatenate(rows, axis=0))
    normed = (unit * gain_ref[...]).astype(jnp.bfloat16)
    gate = product(normed, gate_turned)
    upper = product(normed, up_turned)
    split = blocks * CAP
    sigma = jax.nn.sigmoid(gate)
    passed = gate * sigma
    hidden = (passed[:split] * upper[:split]).astype(jnp.bfloat16)
    to_up_ref[...] = passed[split:]
    to_gate_ref[...] = (upper * sigma * (1.0 + gate * (1.0 - sigma)))[split:]
    give((kept_ref, given_ref), product(hidden, down_ref.at[0]).astype(jnp.bfloat16))


def expert_backward(blocks, *refs):
    gain_ref, to_gate_ref, to_up_ref, gate_ref, up_ref, down_turned = refs[blocks : blocks + 6]
    grads = jnp.concatenate([ref[2 * CAP :] for ref in refs[:blocks]], axis=0)
    hidden_grad = wide_product(grads, down_turned)
    gate_grad = (hidden_grad * to_gate_ref[...]).astype(jnp.bfloat16)
    upper_grad = (hidden_grad * to_up_ref[...]).astype(jnp.bfloat16)
    total = wide_product(gate_grad, gate_ref.at[0]) + wide_product(upper_grad, up_ref.at[0])
    rows = jnp.concatenate([ref[CAP : 2 * CAP] for ref in refs[:blocks]], axis=0)
    unit, scale = unit_rows(rows)
    scaled = total * gain_ref[...]
    inner = jnp.mean(scaled * unit, axis=-1, keepdims=True)
    give(refs[blocks + 6 :], (scale * (scaled - unit * inner)).astype(jnp.bfloat16))


def sent_out(out_hbm, held_ref, sem, columns):
    width = held_ref.shape[1]
    size = width // OUT_PIECES
    copies = []
    for piece in range(OUT_PIECES):
        span = pl.ds(piece * size, size)
        held_ref[:, span] = columns(span).astype(jnp.bfloat16)
        copy = pltpu.make_async_copy(
            held_ref.at[:, span], out_hbm.at[0, :, span], sem.at[piece]
        )
        copy.start()
        copies.append(copy)
    for copy in copies:
        copy.wait()


def combine_forward(early_ref, own_ref, other_ref, out_hbm, held_ref, sem):
    table = early_ref[:, held_ref.shape[1] :]
    picks = []
    for e in range(EF):
        column = EF * CAP + 3 * e
        weight = jnp.sum(
            table[:, column : column + 3].astype(jnp.float32), axis=1, keepdims=True
        )
        picks.append((table[:, e * CAP : (e + 1) * CAP], weight))

    def columns(span):
        total = early_ref[:, span].astype(jnp.float32)
        for (pick, weight), part_ref in zip(picks, (own_ref, other_ref)):
            total = total + weight * product(pick, part_ref.at[:, span])
        return total

    sent_out(out_hbm, held_ref, sem, columns)


def combine_backward(early_ref, own_ref, other_ref, out_hbm, held_ref, sem):
    width = held_ref.shape[1]
    pick = early_ref[:, width : width + EF * CAP]

    def columns(span):
        parts = jnp.concatenate([own_ref[:, span], other_ref[:, span]], axis=0)
        total = jnp.dot(pick, parts, preferred_element_type=jnp.float32)
        return early_ref[:, span].astype(jnp.float32) + total

    sent_out(out_hbm, held_ref, sem, columns)


def on_device(
    sections,
    devices,
    forward_input,
    forward_routes,
    forward_shares,
    backward_input,
    backward_routes,
    backward_shares,
    output_grad,
    norm_gain,
    gate_weight,
    up_weight,
    down_weight,
):
    half = devices // EF
    tokens, width = forward_input.shape[1:]
    hidden = gate_weight.shape[1]
    owner = (lax.axis_index("expert") // half).astype(jnp.int32)[None]

    def swapped(block, k):
        return lax.ppermute(block, "expert", [(i, i ^ k) for i in range(devices)])

    def moved(block, distance):
        route = [(i, (i + distance) % sections) for i in range(sections)]
        return lax.ppermute(block, "section", route)

    def returned(block, distance, k):
        route = [
            (s * devices + z, (s + distance) % sections * devices + (z ^ k))
            for s in range(sections)
            for z in range(devices)
        ]
        return lax.ppermute(block, ("section", "expert"), route)

    def gathered(own, other, held):
        blocks = [own]
        far = [swapped(other, half)]
        step = 1
        while step < half:
            blocks = blocks + [swapped(b, step) for b in blocks]
            far, blocks, *held = lax.optimization_barrier((far, blocks, *held))
            far = far + [swapped(b, step) for b in far]
            step *= 2
        return blocks + far, held

    dispatch_bytes = 3 * tokens * width * 2
    lists = forward_routes.shape[:0:-1]
    groups = (forward_routes, forward_shares, backward_routes, backward_shares)
    layers = (forward_input, backward_input, output_grad)
    own, other, table_f, table_b = call(
        dispatch,
        [bf16((3 * CAP, width))] * 2
        + [jax.ShapeDtypeStruct((n, tokens), jnp.float32) for n in (EF * CAP + 8, EF * CAP)],
        [SMEM] + [ANY] * 7,
        6 * EF * CAP * tokens * width,
        dispatch_bytes,
        24,
        [pltpu.VMEM((1, *lists), a.dtype) for a in groups]
        + [pltpu.VMEM((1, tokens, width), jnp.bfloat16)] * 3
        + [pltpu.SemaphoreType.DMA((7,))],
    )(owner, *(in_hbm(jnp.swapaxes(a, 1, 2)) for a in groups), *(in_hbm(a) for a in layers))

    weights = (gate_weight, up_weight, down_weight)
    pieces = 3 if hidden % (3 * LANES) == 0 else 1
    early_f, early_b, *held = call(
        functools.partial(load, pieces),
        [bf16((tokens, width + LANES))] * 2
        + [pltpu.VMEM(w.shape, w.dtype) for w in weights]
        + [pltpu.VMEM((width, hidden), w.dtype) for w in weights],
        [ANY] * 2 + [VMEM] * 2 + [ANY] * 3,
        0,
        12 * hidden * width * 2,
        8,
        [pltpu.SemaphoreType.DMA((2,)), pltpu.SemaphoreType.DMA((3 * pieces,))],
    )(
        in_hbm(forward_input),
        in_hbm(output_grad),
        table_f,
        table_b,
        *(in_hbm(w) for w in weights),
    )
    early_b = moved(early_b, -1)
    early_f = moved(early_f, 1)
    blocks, held = gathered(own, other, held)
    gate, up, down, gate_turned, up_turned, down_turned = held

    rows = devices * CAP
    weight_bytes = 3 * hidden * width * 2
    outs = [bf16((rows // 2, width))] * 2
    factor = jax.ShapeDtypeStruct((rows, hidden), jnp.float32)
    *parts_f, to_gate, to_up = call(
        functools.partial(expert_forward, devices),
        outs + [factor] * 2,
        [VMEM] * (devices + 4),
        10 * rows * hidden * width,
        weight_bytes,
        16,
    )(*blocks, norm_gain, gate_turned, up_turned, down)
    parts_b = call(
        functools.partial(expert_backward, devices),
        outs,
        [VMEM] * (devices + 6),
        6 * rows * hidden * width,
        weight_bytes,
        16,
    )(*blocks, norm_gain, to_gate, to_up, gate, up, down_turned)

    def handed_back(kept, given, distance):
        step = 1
        while step < half:
            quarter = kept.shape[0] // 2
            kept, given = call(
                add_received,
                [bf16((quarter, width))] * 2,
                [VMEM] * 2,
                0,
                6 * kept.shape[0] * width,
                8,
            )(kept, swapped(given, step))
            step *= 2
        return returned(kept, distance, 0), returned(given, distance, half)

    parts_f = handed_back(*parts_f, 1)
    parts_b = handed_back(*parts_b, -1)
    result = [bf16((1, tokens, width))]
    combine_flops = 2 * tokens * EF * CAP * width
    scratch = [pltpu.VMEM((tokens, width), jnp.bfloat16), pltpu.SemaphoreType.DMA((OUT_PIECES,))]
    (next_input,) = call(
        combine_forward, result, [VMEM] * 3, combine_flops, dispatch_bytes, 16, scratch, ANY
    )(early_f, *parts_f)
    (previous_gradient,) = call(
        combine_backward, result, [VMEM] * 3, combine_flops, dispatch_bytes, 16, scratch, ANY
    )(early_b, *parts_b)
    return next_input, previous_gradient


def solution(mesh):
    rows = P("section", "expert", None)
    return jax.shard_map(
        functools.partial(on_device, mesh.shape["section"], mesh.shape["expert"]),
        mesh=mesh,
        in_specs=(rows,) * 7 + (P("section", None),) + (rows,) * 3,
        out_specs=(rows, rows),
        check_vma=False,
    )
```

```python
import functools

import jax
import jax.numpy as jnp
from jax import lax
from jax.experimental import pallas as pl
from jax.experimental.pallas import tpu as pltpu
from jax.sharding import PartitionSpec as P

EF = 2
CAP = 16
EPSILON = 1e-06
OUT_PIECES = 4
LANES = 128
MIB = 1 << 20

VMEM = pl.BlockSpec(memory_space=pltpu.VMEM)
SMEM = pl.BlockSpec(memory_space=pltpu.SMEM)


ANY = pl.BlockSpec(memory_space=pl.ANY)


def call(body, outs, specs, flops, nbytes, limit, scratch=(), out_spec=VMEM):
    return pl.pallas_call(
        body,
        out_shape=outs,
        in_specs=specs,
        out_specs=[out_spec] * len(outs),
        scratch_shapes=scratch,
        compiler_params=pltpu.CompilerParams(vmem_limit_bytes=limit * MIB),
        cost_estimate=pl.CostEstimate(flops=flops, bytes_accessed=nbytes, transcendentals=0),
    )


def bf16(shape):
    return jax.ShapeDtypeStruct(shape, jnp.bfloat16)


def in_hbm(array):
    return pltpu.with_memory_space_constraint(array, pltpu.HBM)


def slot_tables(owner, groups):
    tokens = groups[0][0].shape[1]
    rows = EF * CAP * len(groups)
    members, weights = [], []
    for routes, shares in groups:
        for expert in (owner, 1 - owner):
            hit = routes == expert
            member = jnp.sum(jnp.where(hit, 1.0, 0.0), axis=0, keepdims=True)
            members.append(jnp.broadcast_to(member, (CAP, tokens)))
            weights.append(jnp.sum(jnp.where(hit, shares, 0.0), axis=0, keepdims=True))
    member = jnp.concatenate(members, axis=0)
    row = lax.broadcasted_iota(jnp.int32, (tokens, tokens), 0)
    col = lax.broadcasted_iota(jnp.int32, (tokens, tokens), 1)
    earlier = jnp.where(row < col, 1.0, 0.0).astype(jnp.bfloat16)
    rank = jnp.dot(member.astype(jnp.bfloat16), earlier, preferred_element_type=jnp.float32)
    place = lax.broadcasted_iota(jnp.int32, (rows, tokens), 0) % CAP
    placed = jnp.where((member > 0.5) & (rank == place.astype(jnp.float32)), 1.0, 0.0)
    return [
        (placed[i * EF * CAP : (i + 1) * EF * CAP], weights[i * EF : (i + 1) * EF])
        for i in range(len(groups))
    ]


def turned(table):
    rows, tokens = table.shape
    return jnp.transpose(jnp.concatenate([table, jnp.zeros((LANES - rows, tokens), jnp.float32)], axis=0))


def started(pairs, sem):
    loads = [pltpu.make_async_copy(src, dst, sem.at[i]) for i, (src, dst) in enumerate(pairs)]
    for load in loads:
        load.start()
    return loads


def dispatch(owner_ref, *refs):
    loads = started(list(zip(refs[:7], refs[11:18])), refs[18])
    own_ref, other_ref, forward_ref, backward_ref = refs[7:11]
    routes_f, shares_f, routes_b, shares_b, rows_f, rows_b, grads = refs[11:18]
    for load in loads[:4]:
        load.wait()
    groups = [(routes_f[0], shares_f[0]), (routes_b[0], shares_b[0])]
    (placed_f, weights_f), (placed_b, weights_b) = slot_tables(owner_ref[0], groups)
    slot = lax.broadcasted_iota(jnp.int32, placed_b.shape, 0)
    share = placed_b * jnp.where(slot < CAP, weights_b[0], weights_b[1])
    share = jnp.sum(share, axis=1, keepdims=True)
    for i, (placed, rows) in enumerate(((placed_f, rows_f), (placed_b, rows_b), (placed_b, grads))):
        loads[4 + i].wait()
        slots = product(placed.astype(jnp.bfloat16), rows.at[0])
        slots = (slots if i < 2 else share * slots).astype(jnp.bfloat16)
        own_ref[i * CAP : (i + 1) * CAP] = slots[:CAP]
        other_ref[i * CAP : (i + 1) * CAP] = slots[CAP:]
    unused = jnp.zeros((8 - EF, placed_f.shape[1]), jnp.float32)
    forward_ref[...] = jnp.concatenate([placed_f, *weights_f, unused], axis=0)
    backward_ref[...] = placed_b


def load(pieces, rows_f, rows_b, table_f, table_b, *refs):
    *refs, early_sem, sem = refs
    count = (len(refs) - 2) // 3
    early_f, early_b = refs[count : count + 2]
    source, held, turned_ref = refs[:count], refs[count + 2 : -count], refs[-count:]
    width = rows_f.shape[2]
    size = held[0].shape[1] // pieces
    spans = [pl.ds(piece * size, size) for piece in range(pieces)]
    pairs = [(src.at[0, span], dst.at[0, span]) for span in spans for src, dst in zip(source, held)]
    loads = started(pairs, sem)
    early = started(
        [(rows_f.at[0], early_f.at[:, :width]), (rows_b.at[0], early_b.at[:, :width])], early_sem
    )
    rows = [table_f[: EF * CAP]]
    for e in range(EF):
        left = table_f[EF * CAP + e : EF * CAP + e + 1]
        for _ in range(3):
            rows.append(left.astype(jnp.bfloat16).astype(jnp.float32))
            left = left - rows[-1]
    rows.append(jnp.zeros((2, left.shape[1]), jnp.float32))
    early_f[:, width:] = turned(jnp.concatenate(rows, axis=0)).astype(jnp.bfloat16)
    early_b[:, width:] = turned(table_b[...]).astype(jnp.bfloat16)
    for piece, span in enumerate(spans):
        for i in range(count):
            loads[piece * count + i].wait()
            turned_ref[i][:, span] = held[i][0, span].T
    for each in early:
        each.wait()


def product(left, right_ref):
    return jnp.dot(left, right_ref[...], preferred_element_type=jnp.float32)


def wide_product(left, right_ref):
    rows, depth = left.shape
    if rows >= LANES:
        return product(left, right_ref)
    below = jnp.zeros((LANES - rows, depth), left.dtype)
    return product(jnp.concatenate([left, below], axis=0), right_ref)[:rows]


def unit_rows(rows):
    values = rows.astype(jnp.float32)
    scale = lax.rsqrt(jnp.mean(values * values, axis=-1, keepdims=True) + EPSILON)
    return values * scale, scale


def halving(blocks):
    bits = blocks.bit_length() - 1
    return sorted(range(blocks), key=lambda k: [k >> b & 1 for b in range(bits)])


def give(outs, rows):
    order = halving(rows.shape[0] // CAP)
    rows = jnp.concatenate([rows[k * CAP : (k + 1) * CAP] for k in order], axis=0)
    split = rows.shape[0] // 2
    outs[0][...] = rows[:split]
    outs[1][...] = rows[split:]


def add_received(kept_ref, received_ref, *outs):
    total = kept_ref[...].astype(jnp.float32) + received_ref[...].astype(jnp.float32)
    total = total.astype(jnp.bfloat16)
    split = total.shape[0] // 2
    outs[0][...] = total[:split]
    outs[1][...] = total[split:]


def normed_rows(rows, gain):
    return (unit_rows(rows)[0] * gain).astype(jnp.bfloat16)


def normalized(*refs):
    gain_ref, out_ref = refs[-2:]
    for k, ref in enumerate(refs[:-2]):
        span = pl.ds(2 * CAP * k, 2 * CAP)
        out_ref[span] = normed_rows(ref[: 2 * CAP], gain_ref[...])


def expert_forward(blocks, last_ref, held_ref, *refs):
    gain_ref, gate_turned, up_turned, down_ref = refs[:4]
    kept_ref, given_ref, gate_ref, upper_ref = refs[4:]
    ready = [held_ref[CAP * k : CAP * (k + 1)] for k in range(2 * blocks - 2)]
    last = normed_rows(last_ref[: 2 * CAP], gain_ref[...])
    normed = jnp.concatenate(ready[::2] + [last[:CAP]] + ready[1::2] + [last[CAP:]], axis=0)
    gate = product(normed, gate_turned)
    upper = product(normed, up_turned)
    split = blocks * CAP
    gate_ref[...] = gate[split:]
    upper_ref[...] = upper[split:]
    gate, upper = gate[:split], upper[:split]
    hidden = (gate * jax.nn.sigmoid(gate) * upper).astype(jnp.bfloat16)
    give((kept_ref, given_ref), wide_product(hidden, down_ref.at[0]).astype(jnp.bfloat16))


def expert_backward(blocks, *refs):
    gain_ref, held_gate, held_upper, gate_ref, up_ref, down_turned = refs[blocks : blocks + 6]
    grads = jnp.concatenate([ref[2 * CAP :] for ref in refs[:blocks]], axis=0)
    hidden_grad = wide_product(grads, down_turned)
    gate, upper = held_gate[...], held_upper[...]
    sigma = jax.nn.sigmoid(gate)
    gate_grad = (hidden_grad * upper * sigma * (1.0 + gate * (1.0 - sigma))).astype(jnp.bfloat16)
    upper_grad = (hidden_grad * gate * sigma).astype(jnp.bfloat16)
    total = wide_product(gate_grad, gate_ref.at[0]) + wide_product(upper_grad, up_ref.at[0])
    rows = jnp.concatenate([ref[CAP : 2 * CAP] for ref in refs[:blocks]], axis=0)
    unit, scale = unit_rows(rows)
    scaled = total * gain_ref[...]
    inner = jnp.mean(scaled * unit, axis=-1, keepdims=True)
    give(refs[blocks + 6 :], (scale * (scaled - unit * inner)).astype(jnp.bfloat16))


def sent_out(out_hbm, held_ref, sem, columns):
    width = held_ref.shape[1]
    size = width // OUT_PIECES
    copies = []
    for piece in range(OUT_PIECES):
        span = pl.ds(piece * size, size)
        held_ref[:, span] = columns(span).astype(jnp.bfloat16)
        copy = pltpu.make_async_copy(
            held_ref.at[:, span], out_hbm.at[0, :, span], sem.at[piece]
        )
        copy.start()
        copies.append(copy)
    for copy in copies:
        copy.wait()


def combine_forward(early_ref, own_ref, other_ref, out_hbm, held_ref, sem):
    table = early_ref[:, held_ref.shape[1] :]
    picks = []
    for e in range(EF):
        column = EF * CAP + 3 * e
        weight = jnp.sum(
            table[:, column : column + 3].astype(jnp.float32), axis=1, keepdims=True
        )
        picks.append((table[:, e * CAP : (e + 1) * CAP], weight))

    def columns(span):
        total = early_ref[:, span].astype(jnp.float32)
        for (pick, weight), part_ref in zip(picks, (own_ref, other_ref)):
            total = total + weight * product(pick, part_ref.at[:, span])
        return total

    sent_out(out_hbm, held_ref, sem, columns)


def combine_backward(early_ref, own_ref, other_ref, out_hbm, held_ref, sem):
    width = held_ref.shape[1]
    pick = early_ref[:, width : width + EF * CAP]

    def columns(span):
        parts = jnp.concatenate([own_ref[:, span], other_ref[:, span]], axis=0)
        total = jnp.dot(pick, parts, preferred_element_type=jnp.float32)
        return early_ref[:, span].astype(jnp.float32) + total

    sent_out(out_hbm, held_ref, sem, columns)


def on_device(
    sections,
    devices,
    forward_input,
    forward_routes,
    forward_shares,
    backward_input,
    backward_routes,
    backward_shares,
    output_grad,
    norm_gain,
    gate_weight,
    up_weight,
    down_weight,
):
    half = devices // EF
    tokens, width = forward_input.shape[1:]
    hidden = gate_weight.shape[1]
    owner = (lax.axis_index("expert") // half).astype(jnp.int32)[None]

    def swapped(block, k):
        return lax.ppermute(block, "expert", [(i, i ^ k) for i in range(devices)])

    def moved(block, distance):
        route = [(i, (i + distance) % sections) for i in range(sections)]
        return lax.ppermute(block, "section", route)

    def returned(block, distance, k):
        route = [
            (s * devices + z, (s + distance) % sections * devices + (z ^ k))
            for s in range(sections)
            for z in range(devices)
        ]
        return lax.ppermute(block, ("section", "expert"), route)

    def gathered(own, other, held):
        blocks = [own]
        far = [swapped(other, half)]
        step = 1
        while step < half:
            blocks = blocks + [swapped(b, step) for b in blocks]
            far, blocks, *held = lax.optimization_barrier((far, blocks, *held))
            far = far + [swapped(b, step) for b in far]
            step *= 2
        return blocks + far, held

    dispatch_bytes = 3 * tokens * width * 2
    lists = forward_routes.shape[:0:-1]
    groups = (forward_routes, forward_shares, backward_routes, backward_shares)
    layers = (forward_input, backward_input, output_grad)
    own, other, table_f, table_b = call(
        dispatch,
        [bf16((3 * CAP, width))] * 2
        + [jax.ShapeDtypeStruct((n, tokens), jnp.float32) for n in (EF * CAP + 8, EF * CAP)],
        [SMEM] + [ANY] * 7,
        6 * EF * CAP * tokens * width,
        dispatch_bytes,
        24,
        [pltpu.VMEM((1, *lists), a.dtype) for a in groups]
        + [pltpu.VMEM((1, tokens, width), jnp.bfloat16)] * 3
        + [pltpu.SemaphoreType.DMA((7,))],
    )(owner, *(in_hbm(jnp.swapaxes(a, 1, 2)) for a in groups), *(in_hbm(a) for a in layers))

    weights = (gate_weight, up_weight, down_weight)
    pieces = 3 if hidden % (3 * LANES) == 0 else 1
    early_f, early_b, *held = call(
        functools.partial(load, pieces),
        [bf16((tokens, width + LANES))] * 2
        + [pltpu.VMEM(w.shape, w.dtype) for w in weights]
        + [pltpu.VMEM((width, hidden), w.dtype) for w in weights],
        [ANY] * 2 + [VMEM] * 2 + [ANY] * 3,
        0,
        12 * hidden * width * 2,
        8,
        [pltpu.SemaphoreType.DMA((2,)), pltpu.SemaphoreType.DMA((3 * pieces,))],
    )(
        in_hbm(forward_input),
        in_hbm(output_grad),
        table_f,
        table_b,
        *(in_hbm(w) for w in weights),
    )
    early_b = moved(early_b, -1)
    early_f = moved(early_f, 1)
    blocks, held = gathered(own, other, held)
    gate, up, down, gate_turned, up_turned, down_turned = held

    rows = devices * CAP
    weight_bytes = 3 * hidden * width * 2
    outs = [bf16((rows // 2, width))] * 2
    (held_rows,) = call(
        normalized,
        [bf16((2 * CAP * (devices - 1), width))],
        [VMEM] * devices,
        0,
        8 * CAP * devices * width,
        16,
    )(*blocks[:-1], norm_gain)
    factor = jax.ShapeDtypeStruct((rows, hidden), jnp.float32)
    *parts_f, gate_b, upper_b = call(
        functools.partial(expert_forward, devices),
        outs + [factor] * 2,
        [VMEM] * 6,
        10 * rows * hidden * width,
        weight_bytes,
        16,
    )(blocks[-1], held_rows, norm_gain, gate_turned, up_turned, down)
    parts_b = call(
        functools.partial(expert_backward, devices),
        outs,
        [VMEM] * (devices + 6),
        6 * rows * hidden * width,
        weight_bytes,
        16,
    )(*blocks, norm_gain, gate_b, upper_b, gate, up, down_turned)

    def handed_back(kept, given, distance):
        step = 1
        while step < half:
            quarter = kept.shape[0] // 2
            kept, given = call(
                add_received,
                [bf16((quarter, width))] * 2,
                [VMEM] * 2,
                0,
                6 * kept.shape[0] * width,
                8,
            )(kept, swapped(given, step))
            step *= 2
        return returned(kept, distance, 0), returned(given, distance, half)

    parts_f = handed_back(*parts_f, 1)
    parts_b = handed_back(*parts_b, -1)
    result = [bf16((1, tokens, width))]
    combine_flops = 2 * tokens * EF * CAP * width
    scratch = [pltpu.VMEM((tokens, width), jnp.bfloat16), pltpu.SemaphoreType.DMA((OUT_PIECES,))]
    (next_input,) = call(
        combine_forward, result, [VMEM] * 3, combine_flops, dispatch_bytes, 16, scratch, ANY
    )(early_f, *parts_f)
    (previous_gradient,) = call(
        combine_backward, result, [VMEM] * 3, combine_flops, dispatch_bytes, 16, scratch, ANY
    )(early_b, *parts_b)
    return next_input, previous_gradient


def solution(mesh):
    rows = P("section", "expert", None)
    return jax.shard_map(
        functools.partial(on_device, mesh.shape["section"], mesh.shape["expert"]),
        mesh=mesh,
        in_specs=(rows,) * 7 + (P("section", None),) + (rows,) * 3,
        out_specs=(rows, rows),
        check_vma=False,
    )
```

```python
import functools

import jax
import jax.numpy as jnp
from jax import lax
from jax.experimental import pallas as pl
from jax.experimental.pallas import tpu as pltpu
from jax.sharding import PartitionSpec as P

EF = 2
CAP = 16
EPSILON = 1e-06
OUT_PIECES = 4
LANES = 128
MIB = 1 << 20

VMEM = pl.BlockSpec(memory_space=pltpu.VMEM)
SMEM = pl.BlockSpec(memory_space=pltpu.SMEM)


ANY = pl.BlockSpec(memory_space=pl.ANY)


def call(body, outs, specs, flops, nbytes, limit, scratch=(), out_spec=VMEM):
    return pl.pallas_call(
        body,
        out_shape=outs,
        in_specs=specs,
        out_specs=[out_spec] * len(outs),
        scratch_shapes=scratch,
        compiler_params=pltpu.CompilerParams(vmem_limit_bytes=limit * MIB),
        cost_estimate=pl.CostEstimate(flops=flops, bytes_accessed=nbytes, transcendentals=0),
    )


def bf16(shape):
    return jax.ShapeDtypeStruct(shape, jnp.bfloat16)


def in_hbm(array):
    return pltpu.with_memory_space_constraint(array, pltpu.HBM)


def slot_tables(owner, groups):
    tokens = groups[0][0].shape[1]
    rows = EF * CAP * len(groups)
    members, weights = [], []
    for routes, shares in groups:
        for expert in (owner, 1 - owner):
            hit = routes == expert
            member = jnp.sum(jnp.where(hit, 1.0, 0.0), axis=0, keepdims=True)
            members.append(jnp.broadcast_to(member, (CAP, tokens)))
            weights.append(jnp.sum(jnp.where(hit, shares, 0.0), axis=0, keepdims=True))
    member = jnp.concatenate(members, axis=0)
    row = lax.broadcasted_iota(jnp.int32, (tokens, tokens), 0)
    col = lax.broadcasted_iota(jnp.int32, (tokens, tokens), 1)
    earlier = jnp.where(row < col, 1.0, 0.0).astype(jnp.bfloat16)
    rank = jnp.dot(member.astype(jnp.bfloat16), earlier, preferred_element_type=jnp.float32)
    place = lax.broadcasted_iota(jnp.int32, (rows, tokens), 0) % CAP
    placed = jnp.where((member > 0.5) & (rank == place.astype(jnp.float32)), 1.0, 0.0)
    return [
        (placed[i * EF * CAP : (i + 1) * EF * CAP], weights[i * EF : (i + 1) * EF])
        for i in range(len(groups))
    ]


def turned(table):
    rows, tokens = table.shape
    return jnp.transpose(jnp.concatenate([table, jnp.zeros((LANES - rows, tokens), jnp.float32)], axis=0))


def started(pairs, sem):
    loads = [pltpu.make_async_copy(src, dst, sem.at[i]) for i, (src, dst) in enumerate(pairs)]
    for load in loads:
        load.start()
    return loads


def dispatch(owner_ref, *refs):
    loads = started(list(zip(refs[:7], refs[11:18])), refs[18])
    own_ref, other_ref, forward_ref, backward_ref = refs[7:11]
    routes_f, shares_f, routes_b, shares_b, rows_f, rows_b, grads = refs[11:18]
    for load in loads[:4]:
        load.wait()
    groups = [(routes_f[0], shares_f[0]), (routes_b[0], shares_b[0])]
    (placed_f, weights_f), (placed_b, weights_b) = slot_tables(owner_ref[0], groups)
    slot = lax.broadcasted_iota(jnp.int32, placed_b.shape, 0)
    share = placed_b * jnp.where(slot < CAP, weights_b[0], weights_b[1])
    share = jnp.sum(share, axis=1, keepdims=True)
    for i, (placed, rows) in enumerate(((placed_f, rows_f), (placed_b, rows_b), (placed_b, grads))):
        loads[4 + i].wait()
        slots = product(placed.astype(jnp.bfloat16), rows.at[0])
        slots = (slots if i < 2 else share * slots).astype(jnp.bfloat16)
        own_ref[i * CAP : (i + 1) * CAP] = slots[:CAP]
        other_ref[i * CAP : (i + 1) * CAP] = slots[CAP:]
    unused = jnp.zeros((8 - EF, placed_f.shape[1]), jnp.float32)
    forward_ref[...] = jnp.concatenate([placed_f, *weights_f, unused], axis=0)
    backward_ref[...] = placed_b


def load(pieces, rows_f, rows_b, table_f, table_b, *refs):
    *refs, early_sem, sem = refs
    count = (len(refs) - 2) // 3
    early_f, early_b = refs[count : count + 2]
    source, held, turned_ref = refs[:count], refs[count + 2 : -count], refs[-count:]
    width = rows_f.shape[2]
    size = held[0].shape[1] // pieces
    spans = [pl.ds(piece * size, size) for piece in range(pieces)]
    pairs = [(src.at[0, span], dst.at[0, span]) for span in spans for src, dst in zip(source, held)]
    loads = started(pairs, sem)
    early = started(
        [(rows_f.at[0], early_f.at[:, :width]), (rows_b.at[0], early_b.at[:, :width])], early_sem
    )
    rows = [table_f[: EF * CAP]]
    for e in range(EF):
        left = table_f[EF * CAP + e : EF * CAP + e + 1]
        for _ in range(3):
            rows.append(left.astype(jnp.bfloat16).astype(jnp.float32))
            left = left - rows[-1]
    rows.append(jnp.zeros((2, left.shape[1]), jnp.float32))
    early_f[:, width:] = turned(jnp.concatenate(rows, axis=0)).astype(jnp.bfloat16)
    early_b[:, width:] = turned(table_b[...]).astype(jnp.bfloat16)
    for piece, span in enumerate(spans):
        for i in range(count):
            loads[piece * count + i].wait()
            turned_ref[i][:, span] = held[i][0, span].T
    for each in early:
        each.wait()


def product(left, right_ref):
    return jnp.dot(left, right_ref[...], preferred_element_type=jnp.float32)


def wide_product(left, right_ref):
    rows, depth = left.shape
    if rows >= LANES:
        return product(left, right_ref)
    below = jnp.zeros((LANES - rows, depth), left.dtype)
    return product(jnp.concatenate([left, below], axis=0), right_ref)[:rows]


def unit_rows(rows):
    values = rows.astype(jnp.float32)
    scale = lax.rsqrt(jnp.mean(values * values, axis=-1, keepdims=True) + EPSILON)
    return values * scale, scale


def halving(blocks):
    bits = blocks.bit_length() - 1
    return sorted(range(blocks), key=lambda k: [k >> b & 1 for b in range(bits)])


def give(outs, rows):
    order = halving(rows.shape[0] // CAP)
    rows = jnp.concatenate([rows[k * CAP : (k + 1) * CAP] for k in order], axis=0)
    split = rows.shape[0] // 2
    outs[0][...] = rows[:split]
    outs[1][...] = rows[split:]


def add_received(kept_ref, received_ref, *outs):
    total = kept_ref[...].astype(jnp.float32) + received_ref[...].astype(jnp.float32)
    total = total.astype(jnp.bfloat16)
    split = total.shape[0] // 2
    outs[0][...] = total[:split]
    outs[1][...] = total[split:]


def normed_rows(rows, gain):
    return (unit_rows(rows)[0] * gain).astype(jnp.bfloat16)


def normalized(*refs):
    gain_ref, out_ref = refs[-2:]
    for k, ref in enumerate(refs[:-2]):
        span = pl.ds(2 * CAP * k, 2 * CAP)
        out_ref[span] = normed_rows(ref[: 2 * CAP], gain_ref[...])


def expert_forward(blocks, last_ref, held_ref, *refs):
    gain_ref, gate_turned, up_turned, down_ref = refs[:4]
    kept_ref, given_ref, gate_ref, upper_ref = refs[4:]
    ready = [held_ref[CAP * k : CAP * (k + 1)] for k in range(2 * blocks - 2)]
    last = normed_rows(last_ref[: 2 * CAP], gain_ref[...])
    normed = jnp.concatenate(ready[::2] + [last[:CAP]] + ready[1::2] + [last[CAP:]], axis=0)
    gate = product(normed, gate_turned)
    upper = product(normed, up_turned)
    split = blocks * CAP
    gate_ref[...] = gate[split:]
    upper_ref[...] = upper[split:]
    gate, upper = gate[:split], upper[:split]
    hidden = (gate * jax.nn.sigmoid(gate) * upper).astype(jnp.bfloat16)
    give((kept_ref, given_ref), product(hidden, down_ref.at[0]).astype(jnp.bfloat16))


def expert_backward(blocks, *refs):
    gain_ref, held_gate, held_upper, gate_ref, up_ref, down_turned = refs[blocks : blocks + 6]
    grads = jnp.concatenate([ref[2 * CAP :] for ref in refs[:blocks]], axis=0)
    hidden_grad = wide_product(grads, down_turned)
    gate, upper = held_gate[...], held_upper[...]
    sigma = jax.nn.sigmoid(gate)
    gate_grad = (hidden_grad * upper * sigma * (1.0 + gate * (1.0 - sigma))).astype(jnp.bfloat16)
    upper_grad = (hidden_grad * gate * sigma).astype(jnp.bfloat16)
    total = wide_product(gate_grad, gate_ref.at[0]) + wide_product(upper_grad, up_ref.at[0])
    rows = jnp.concatenate([ref[CAP : 2 * CAP] for ref in refs[:blocks]], axis=0)
    unit, scale = unit_rows(rows)
    scaled = total * gain_ref[...]
    inner = jnp.mean(scaled * unit, axis=-1, keepdims=True)
    give(refs[blocks + 6 :], (scale * (scaled - unit * inner)).astype(jnp.bfloat16))


def sent_out(out_hbm, held_ref, sem, columns):
    width = held_ref.shape[1]
    size = width // OUT_PIECES
    copies = []
    for piece in range(OUT_PIECES):
        span = pl.ds(piece * size, size)
        held_ref[:, span] = columns(span).astype(jnp.bfloat16)
        copy = pltpu.make_async_copy(
            held_ref.at[:, span], out_hbm.at[0, :, span], sem.at[piece]
        )
        copy.start()
        copies.append(copy)
    for copy in copies:
        copy.wait()


def combine_forward(early_ref, own_ref, other_ref, out_hbm, held_ref, sem):
    table = early_ref[:, held_ref.shape[1] :]
    picks = []
    for e in range(EF):
        column = EF * CAP + 3 * e
        weight = jnp.sum(
            table[:, column : column + 3].astype(jnp.float32), axis=1, keepdims=True
        )
        picks.append((table[:, e * CAP : (e + 1) * CAP], weight))

    def columns(span):
        total = early_ref[:, span].astype(jnp.float32)
        for (pick, weight), part_ref in zip(picks, (own_ref, other_ref)):
            total = total + weight * product(pick, part_ref.at[:, span])
        return total

    sent_out(out_hbm, held_ref, sem, columns)


def combine_backward(early_ref, own_ref, other_ref, out_hbm, held_ref, sem):
    width = held_ref.shape[1]
    pick = early_ref[:, width : width + EF * CAP]

    def columns(span):
        parts = jnp.concatenate([own_ref[:, span], other_ref[:, span]], axis=0)
        total = jnp.dot(pick, parts, preferred_element_type=jnp.float32)
        return early_ref[:, span].astype(jnp.float32) + total

    sent_out(out_hbm, held_ref, sem, columns)


def on_device(
    sections,
    devices,
    forward_input,
    forward_routes,
    forward_shares,
    backward_input,
    backward_routes,
    backward_shares,
    output_grad,
    norm_gain,
    gate_weight,
    up_weight,
    down_weight,
):
    half = devices // EF
    tokens, width = forward_input.shape[1:]
    hidden = gate_weight.shape[1]
    owner = (lax.axis_index("expert") // half).astype(jnp.int32)[None]

    def swapped(block, k):
        return lax.ppermute(block, "expert", [(i, i ^ k) for i in range(devices)])

    def moved(block, distance):
        route = [(i, (i + distance) % sections) for i in range(sections)]
        return lax.ppermute(block, "section", route)

    def returned(block, distance, k):
        route = [
            (s * devices + z, (s + distance) % sections * devices + (z ^ k))
            for s in range(sections)
            for z in range(devices)
        ]
        return lax.ppermute(block, ("section", "expert"), route)

    def gathered(own, other, held):
        blocks = [own]
        far = [swapped(other, half)]
        step = 1
        while step < half:
            blocks = blocks + [swapped(b, step) for b in blocks]
            far, blocks, *held = lax.optimization_barrier((far, blocks, *held))
            far = far + [swapped(b, step) for b in far]
            step *= 2
        return blocks + far, held

    dispatch_bytes = 3 * tokens * width * 2
    lists = forward_routes.shape[:0:-1]
    groups = (forward_routes, forward_shares, backward_routes, backward_shares)
    layers = (forward_input, backward_input, output_grad)
    own, other, table_f, table_b = call(
        dispatch,
        [bf16((3 * CAP, width))] * 2
        + [jax.ShapeDtypeStruct((n, tokens), jnp.float32) for n in (EF * CAP + 8, EF * CAP)],
        [SMEM] + [ANY] * 7,
        6 * EF * CAP * tokens * width,
        dispatch_bytes,
        24,
        [pltpu.VMEM((1, *lists), a.dtype) for a in groups]
        + [pltpu.VMEM((1, tokens, width), jnp.bfloat16)] * 3
        + [pltpu.SemaphoreType.DMA((7,))],
    )(owner, *(in_hbm(jnp.swapaxes(a, 1, 2)) for a in groups), *(in_hbm(a) for a in layers))

    weights = (gate_weight, up_weight, down_weight)
    pieces = 3 if hidden % (3 * LANES) == 0 else 1
    early_f, early_b, *held = call(
        functools.partial(load, pieces),
        [bf16((tokens, width + LANES))] * 2
        + [pltpu.VMEM(w.shape, w.dtype) for w in weights]
        + [pltpu.VMEM((width, hidden), w.dtype) for w in weights],
        [ANY] * 2 + [VMEM] * 2 + [ANY] * 3,
        0,
        12 * hidden * width * 2,
        8,
        [pltpu.SemaphoreType.DMA((2,)), pltpu.SemaphoreType.DMA((3 * pieces,))],
    )(
        in_hbm(forward_input),
        in_hbm(output_grad),
        table_f,
        table_b,
        *(in_hbm(w) for w in weights),
    )
    early_b = moved(early_b, -1)
    early_f = moved(early_f, 1)
    blocks, held = gathered(own, other, held)
    gate, up, down, gate_turned, up_turned, down_turned = held

    rows = devices * CAP
    weight_bytes = 3 * hidden * width * 2
    outs = [bf16((rows // 2, width))] * 2
    (held_rows,) = call(
        normalized,
        [bf16((2 * CAP * (devices - 1), width))],
        [VMEM] * devices,
        0,
        8 * CAP * devices * width,
        16,
    )(*blocks[:-1], norm_gain)
    factor = jax.ShapeDtypeStruct((rows, hidden), jnp.float32)
    *parts_f, gate_b, upper_b = call(
        functools.partial(expert_forward, devices),
        outs + [factor] * 2,
        [VMEM] * 6,
        10 * rows * hidden * width,
        weight_bytes,
        16,
    )(blocks[-1], held_rows, norm_gain, gate_turned, up_turned, down)
    parts_b = call(
        functools.partial(expert_backward, devices),
        outs,
        [VMEM] * (devices + 6),
        6 * rows * hidden * width,
        weight_bytes,
        16,
    )(*blocks, norm_gain, gate_b, upper_b, gate, up, down_turned)

    def handed_back(kept, given, distance):
        step = 1
        while step < half:
            quarter = kept.shape[0] // 2
            kept, given = call(
                add_received,
                [bf16((quarter, width))] * 2,
                [VMEM] * 2,
                0,
                6 * kept.shape[0] * width,
                8,
            )(kept, swapped(given, step))
            step *= 2
        return returned(kept, distance, 0), returned(given, distance, half)

    parts_f = handed_back(*parts_f, 1)
    parts_b = handed_back(*parts_b, -1)
    result = [bf16((1, tokens, width))]
    combine_flops = 2 * tokens * EF * CAP * width
    scratch = [pltpu.VMEM((tokens, width), jnp.bfloat16), pltpu.SemaphoreType.DMA((OUT_PIECES,))]
    (next_input,) = call(
        combine_forward, result, [VMEM] * 3, combine_flops, dispatch_bytes, 16, scratch, ANY
    )(early_f, *parts_f)
    (previous_gradient,) = call(
        combine_backward, result, [VMEM] * 3, combine_flops, dispatch_bytes, 16, scratch, ANY
    )(early_b, *parts_b)
    return next_input, previous_gradient


def solution(mesh):
    rows = P("section", "expert", None)
    return jax.shard_map(
        functools.partial(on_device, mesh.shape["section"], mesh.shape["expert"]),
        mesh=mesh,
        in_specs=(rows,) * 7 + (P("section", None),) + (rows,) * 3,
        out_specs=(rows, rows),
        check_vma=False,
    )
```

```python
import functools

import jax
import jax.numpy as jnp
from jax import lax
from jax.experimental import pallas as pl
from jax.experimental.pallas import tpu as pltpu
from jax.sharding import PartitionSpec as P

EF = 2
CAP = 16
EPSILON = 1e-06
OUT_PIECES = 2
LANES = 128
MIB = 1 << 20

VMEM = pl.BlockSpec(memory_space=pltpu.VMEM)
SMEM = pl.BlockSpec(memory_space=pltpu.SMEM)


ANY = pl.BlockSpec(memory_space=pl.ANY)


def call(body, outs, specs, flops, nbytes, limit, scratch=(), out_spec=VMEM):
    return pl.pallas_call(
        body,
        out_shape=outs,
        in_specs=specs,
        out_specs=[out_spec] * len(outs),
        scratch_shapes=scratch,
        compiler_params=pltpu.CompilerParams(vmem_limit_bytes=limit * MIB),
        cost_estimate=pl.CostEstimate(flops=flops, bytes_accessed=nbytes, transcendentals=0),
    )


def bf16(shape):
    return jax.ShapeDtypeStruct(shape, jnp.bfloat16)


def in_hbm(array):
    return pltpu.with_memory_space_constraint(array, pltpu.HBM)


def slot_tables(owner, groups):
    tokens = groups[0][0].shape[1]
    rows = EF * CAP * len(groups)
    members, weights = [], []
    for routes, shares in groups:
        for expert in (owner, 1 - owner):
            hit = routes == expert
            member = jnp.sum(jnp.where(hit, 1.0, 0.0), axis=0, keepdims=True)
            members.append(jnp.broadcast_to(member, (CAP, tokens)))
            weights.append(jnp.sum(jnp.where(hit, shares, 0.0), axis=0, keepdims=True))
    member = jnp.concatenate(members, axis=0)
    row = lax.broadcasted_iota(jnp.int32, (tokens, tokens), 0)
    col = lax.broadcasted_iota(jnp.int32, (tokens, tokens), 1)
    earlier = jnp.where(row < col, 1.0, 0.0).astype(jnp.bfloat16)
    rank = jnp.dot(member.astype(jnp.bfloat16), earlier, preferred_element_type=jnp.float32)
    place = lax.broadcasted_iota(jnp.int32, (rows, tokens), 0) % CAP
    placed = jnp.where((member > 0.5) & (rank == place.astype(jnp.float32)), 1.0, 0.0)
    return [
        (placed[i * EF * CAP : (i + 1) * EF * CAP], weights[i * EF : (i + 1) * EF])
        for i in range(len(groups))
    ]


def turned(table):
    rows, tokens = table.shape
    return jnp.transpose(jnp.concatenate([table, jnp.zeros((LANES - rows, tokens), jnp.float32)], axis=0))


def started(pairs, sem):
    loads = [pltpu.make_async_copy(src, dst, sem.at[i]) for i, (src, dst) in enumerate(pairs)]
    for load in loads:
        load.start()
    return loads


def dispatch(owner_ref, *refs):
    loads = started(list(zip(refs[:7], refs[11:18])), refs[18])
    own_ref, other_ref, forward_ref, backward_ref = refs[7:11]
    routes_f, shares_f, routes_b, shares_b, rows_f, rows_b, grads = refs[11:18]
    for load in loads[:4]:
        load.wait()
    groups = [(routes_f[0], shares_f[0]), (routes_b[0], shares_b[0])]
    (placed_f, weights_f), (placed_b, weights_b) = slot_tables(owner_ref[0], groups)
    slot = lax.broadcasted_iota(jnp.int32, placed_b.shape, 0)
    share = placed_b * jnp.where(slot < CAP, weights_b[0], weights_b[1])
    share = jnp.sum(share, axis=1, keepdims=True)
    for i, (placed, rows) in enumerate(((placed_f, rows_f), (placed_b, rows_b), (placed_b, grads))):
        loads[4 + i].wait()
        slots = product(placed.astype(jnp.bfloat16), rows.at[0])
        slots = (slots if i < 2 else share * slots).astype(jnp.bfloat16)
        own_ref[i * CAP : (i + 1) * CAP] = slots[:CAP]
        other_ref[i * CAP : (i + 1) * CAP] = slots[CAP:]
    unused = jnp.zeros((8 - EF, placed_f.shape[1]), jnp.float32)
    forward_ref[...] = jnp.concatenate([placed_f, *weights_f, unused], axis=0)
    backward_ref[...] = placed_b


def load(pieces, rows_f, rows_b, table_f, table_b, *refs):
    *refs, early_sem, sem = refs
    count = (len(refs) - 2) // 3
    early_f, early_b = refs[count : count + 2]
    source, held, turned_ref = refs[:count], refs[count + 2 : -count], refs[-count:]
    width = rows_f.shape[2]
    size = held[0].shape[1] // pieces
    spans = [pl.ds(piece * size, size) for piece in range(pieces)]
    pairs = [(src.at[0, span], dst.at[0, span]) for span in spans for src, dst in zip(source, held)]
    loads = started(pairs, sem)
    early = started(
        [(rows_f.at[0], early_f.at[:, :width]), (rows_b.at[0], early_b.at[:, :width])], early_sem
    )
    rows = [table_f[: EF * CAP]]
    for e in range(EF):
        left = table_f[EF * CAP + e : EF * CAP + e + 1]
        for _ in range(3):
            rows.append(left.astype(jnp.bfloat16).astype(jnp.float32))
            left = left - rows[-1]
    rows.append(jnp.zeros((2, left.shape[1]), jnp.float32))
    early_f[:, width:] = turned(jnp.concatenate(rows, axis=0)).astype(jnp.bfloat16)
    early_b[:, width:] = turned(table_b[...]).astype(jnp.bfloat16)
    for piece, span in enumerate(spans):
        for i in range(count):
            loads[piece * count + i].wait()
            turned_ref[i][:, span] = held[i][0, span].T
    for each in early:
        each.wait()


def product(left, right_ref):
    return jnp.dot(left, right_ref[...], preferred_element_type=jnp.float32)


def wide_product(left, right_ref):
    rows, depth = left.shape
    if rows >= LANES:
        return product(left, right_ref)
    below = jnp.zeros((LANES - rows, depth), left.dtype)
    return product(jnp.concatenate([left, below], axis=0), right_ref)[:rows]


def unit_rows(rows):
    values = rows.astype(jnp.float32)
    scale = lax.rsqrt(jnp.mean(values * values, axis=-1, keepdims=True) + EPSILON)
    return values * scale, scale


def halving(blocks):
    bits = blocks.bit_length() - 1
    return sorted(range(blocks), key=lambda k: [k >> b & 1 for b in range(bits)])


def give(outs, rows):
    order = halving(rows.shape[0] // CAP)
    rows = jnp.concatenate([rows[k * CAP : (k + 1) * CAP] for k in order], axis=0)
    split = rows.shape[0] // 2
    outs[0][...] = rows[:split]
    outs[1][...] = rows[split:]


def add_received(kept_ref, received_ref, *outs):
    total = kept_ref[...].astype(jnp.float32) + received_ref[...].astype(jnp.float32)
    total = total.astype(jnp.bfloat16)
    split = total.shape[0] // 2
    outs[0][...] = total[:split]
    outs[1][...] = total[split:]


def expert_forward(blocks, *refs):
    gain_ref, gate_turned, up_turned, down_ref = refs[blocks : blocks + 4]
    kept_ref, given_ref, to_gate_ref, to_up_ref = refs[blocks + 4 :]
    rows = [ref[:CAP] for ref in refs[:blocks]] + [ref[CAP : 2 * CAP] for ref in refs[:blocks]]
    unit, _ = unit_rows(jnp.concatenate(rows, axis=0))
    normed = (unit * gain_ref[...]).astype(jnp.bfloat16)
    gate = product(normed, gate_turned)
    upper = product(normed, up_turned)
    split = blocks * CAP
    sigma = jax.nn.sigmoid(gate)
    passed = gate * sigma
    hidden = (passed[:split] * upper[:split]).astype(jnp.bfloat16)
    to_up_ref[...] = passed[split:]
    to_gate_ref[...] = (upper * sigma * (1.0 + gate * (1.0 - sigma)))[split:]
    give((kept_ref, given_ref), product(hidden, down_ref.at[0]).astype(jnp.bfloat16))


def expert_backward(blocks, *refs):
    gain_ref, to_gate_ref, to_up_ref, gate_ref, up_ref, down_turned = refs[blocks : blocks + 6]
    grads = jnp.concatenate([ref[2 * CAP :] for ref in refs[:blocks]], axis=0)
    hidden_grad = wide_product(grads, down_turned)
    gate_grad = (hidden_grad * to_gate_ref[...]).astype(jnp.bfloat16)
    upper_grad = (hidden_grad * to_up_ref[...]).astype(jnp.bfloat16)
    total = wide_product(gate_grad, gate_ref.at[0]) + wide_product(upper_grad, up_ref.at[0])
    rows = jnp.concatenate([ref[CAP : 2 * CAP] for ref in refs[:blocks]], axis=0)
    unit, scale = unit_rows(rows)
    scaled = total * gain_ref[...]
    inner = jnp.mean(scaled * unit, axis=-1, keepdims=True)
    give(refs[blocks + 6 :], (scale * (scaled - unit * inner)).astype(jnp.bfloat16))


def sent_out(out_hbm, held_ref, sem, columns):
    width = held_ref.shape[1]
    size = width // OUT_PIECES
    copies = []
    for piece in range(OUT_PIECES):
        span = pl.ds(piece * size, size)
        held_ref[:, span] = columns(span).astype(jnp.bfloat16)
        copy = pltpu.make_async_copy(
            held_ref.at[:, span], out_hbm.at[0, :, span], sem.at[piece]
        )
        copy.start()
        copies.append(copy)
    for copy in copies:
        copy.wait()


def combine_forward(early_ref, own_ref, other_ref, out_hbm, held_ref, sem):
    table = early_ref[:, held_ref.shape[1] :]
    picks = []
    for e in range(EF):
        column = EF * CAP + 3 * e
        weight = jnp.sum(
            table[:, column : column + 3].astype(jnp.float32), axis=1, keepdims=True
        )
        picks.append((table[:, e * CAP : (e + 1) * CAP], weight))

    def columns(span):
        total = early_ref[:, span].astype(jnp.float32)
        for (pick, weight), part_ref in zip(picks, (own_ref, other_ref)):
            total = total + weight * product(pick, part_ref.at[:, span])
        return total

    sent_out(out_hbm, held_ref, sem, columns)


def combine_backward(early_ref, own_ref, other_ref, out_hbm, held_ref, sem):
    width = held_ref.shape[1]
    pick = early_ref[:, width : width + EF * CAP]

    def columns(span):
        parts = jnp.concatenate([own_ref[:, span], other_ref[:, span]], axis=0)
        total = jnp.dot(pick, parts, preferred_element_type=jnp.float32)
        return early_ref[:, span].astype(jnp.float32) + total

    sent_out(out_hbm, held_ref, sem, columns)


def on_device(
    sections,
    devices,
    forward_input,
    forward_routes,
    forward_shares,
    backward_input,
    backward_routes,
    backward_shares,
    output_grad,
    norm_gain,
    gate_weight,
    up_weight,
    down_weight,
):
    half = devices // EF
    tokens, width = forward_input.shape[1:]
    hidden = gate_weight.shape[1]
    owner = (lax.axis_index("expert") // half).astype(jnp.int32)[None]

    def swapped(block, k):
        return lax.ppermute(block, "expert", [(i, i ^ k) for i in range(devices)])

    def moved(block, distance):
        route = [(i, (i + distance) % sections) for i in range(sections)]
        return lax.ppermute(block, "section", route)

    def returned(block, distance, k):
        route = [
            (s * devices + z, (s + distance) % sections * devices + (z ^ k))
            for s in range(sections)
            for z in range(devices)
        ]
        return lax.ppermute(block, ("section", "expert"), route)

    def gathered(own, other, held):
        blocks = [own]
        far = [swapped(other, half)]
        step = 1
        while step < half:
            blocks = blocks + [swapped(b, step) for b in blocks]
            far, blocks, *held = lax.optimization_barrier((far, blocks, *held))
            far = far + [swapped(b, step) for b in far]
            step *= 2
        return blocks + far, held

    dispatch_bytes = 3 * tokens * width * 2
    lists = forward_routes.shape[:0:-1]
    groups = (forward_routes, forward_shares, backward_routes, backward_shares)
    layers = (forward_input, backward_input, output_grad)
    own, other, table_f, table_b = call(
        dispatch,
        [bf16((3 * CAP, width))] * 2
        + [jax.ShapeDtypeStruct((n, tokens), jnp.float32) for n in (EF * CAP + 8, EF * CAP)],
        [SMEM] + [ANY] * 7,
        6 * EF * CAP * tokens * width,
        dispatch_bytes,
        24,
        [pltpu.VMEM((1, *lists), a.dtype) for a in groups]
        + [pltpu.VMEM((1, tokens, width), jnp.bfloat16)] * 3
        + [pltpu.SemaphoreType.DMA((7,))],
    )(owner, *(in_hbm(jnp.swapaxes(a, 1, 2)) for a in groups), *(in_hbm(a) for a in layers))

    weights = (gate_weight, up_weight, down_weight)
    pieces = 3 if hidden % (3 * LANES) == 0 else 1
    early_f, early_b, *held = call(
        functools.partial(load, pieces),
        [bf16((tokens, width + LANES))] * 2
        + [pltpu.VMEM(w.shape, w.dtype) for w in weights]
        + [pltpu.VMEM((width, hidden), w.dtype) for w in weights],
        [ANY] * 2 + [VMEM] * 2 + [ANY] * 3,
        0,
        12 * hidden * width * 2,
        8,
        [pltpu.SemaphoreType.DMA((2,)), pltpu.SemaphoreType.DMA((3 * pieces,))],
    )(
        in_hbm(forward_input),
        in_hbm(output_grad),
        table_f,
        table_b,
        *(in_hbm(w) for w in weights),
    )
    early_b = moved(early_b, -1)
    early_f = moved(early_f, 1)
    blocks, held = gathered(own, other, held)
    gate, up, down, gate_turned, up_turned, down_turned = held

    rows = devices * CAP
    weight_bytes = 3 * hidden * width * 2
    outs = [bf16((rows // 2, width))] * 2
    factor = jax.ShapeDtypeStruct((rows, hidden), jnp.float32)
    *parts_f, to_gate, to_up = call(
        functools.partial(expert_forward, devices),
        outs + [factor] * 2,
        [VMEM] * (devices + 4),
        10 * rows * hidden * width,
        weight_bytes,
        16,
    )(*blocks, norm_gain, gate_turned, up_turned, down)
    parts_b = call(
        functools.partial(expert_backward, devices),
        outs,
        [VMEM] * (devices + 6),
        6 * rows * hidden * width,
        weight_bytes,
        16,
    )(*blocks, norm_gain, to_gate, to_up, gate, up, down_turned)

    def handed_back(kept, given, distance):
        step = 1
        while step < half:
            quarter = kept.shape[0] // 2
            kept, given = call(
                add_received,
                [bf16((quarter, width))] * 2,
                [VMEM] * 2,
                0,
                6 * kept.shape[0] * width,
                8,
            )(kept, swapped(given, step))
            step *= 2
        return returned(kept, distance, 0), returned(given, distance, half)

    parts_f = handed_back(*parts_f, 1)
    parts_b = handed_back(*parts_b, -1)
    result = [bf16((1, tokens, width))]
    combine_flops = 2 * tokens * EF * CAP * width
    scratch = [pltpu.VMEM((tokens, width), jnp.bfloat16), pltpu.SemaphoreType.DMA((OUT_PIECES,))]
    (next_input,) = call(
        combine_forward, result, [VMEM] * 3, combine_flops, dispatch_bytes, 16, scratch, ANY
    )(early_f, *parts_f)
    (previous_gradient,) = call(
        combine_backward, result, [VMEM] * 3, combine_flops, dispatch_bytes, 16, scratch, ANY
    )(early_b, *parts_b)
    return next_input, previous_gradient


def solution(mesh):
    rows = P("section", "expert", None)
    return jax.shard_map(
        functools.partial(on_device, mesh.shape["section"], mesh.shape["expert"]),
        mesh=mesh,
        in_specs=(rows,) * 7 + (P("section", None),) + (rows,) * 3,
        out_specs=(rows, rows),
        check_vma=False,
    )
```
